128 devices in a mesh: row: 16 (over y_hi, x, core), col: 8 (over z, y_lo).
Axes of the slice: x: 4, y: 4 (y_hi: 2, y_lo: 2; y = y_hi * 2 + y_lo), z: 4, core: 2. Of those that a mesh axis runs over, the one named last changes fastest.
Arguments:
- features: bfloat16 [65536, 512], P(('row', 'col')), may hold values from -6 to 6
- weight: bfloat16 [512, 512], replicated, may hold values from -0.25 to 0.25
- bias: float32 [512], replicated, may hold values from -3 to 3
- cotangent: bfloat16 [65536, 512], P(('row', 'col')), may hold values from -6 to 6
- tile_values: bfloat16 [16, 8, 64, 128, 128], P('row', 'col'), may hold values from -0.1875 to 0.1875
- tile_rows: int32 [16, 8, 64], P('row', 'col'), may hold values from 0 to 511, as said below
- tile_cols: int32 [16, 8, 64], P('row', 'col'), may hold values from 0 to 511, as said below
- tile_counts: int32 [16, 8], P('row', 'col'), may hold values from 1 to 64
Outputs:
- output: bfloat16 [65536, 512], P(('row', 'col'))
- feature_grad: bfloat16 [65536, 512], P(('row', 'col'))
- weight_grad: float32 [512, 512], replicated
- bias_grad: float32 [512], replicated
The draws below stay inside these ranges and needn't reach their ends.
Inputs may be any that keep to these rules, and one draw needn't show every extreme that they name: `tile_rows`: A tile on device (p, q) has its row block in row group p, that is row block // 32 == p, and its column block's atoms on devices of index q along col, that is (column block // 4) % 8 == q. The rows of features held by device (p, q) are blocks p * 4 * 8 + q * 4 to that plus 4 - 1. Row and column pairs may repeat. `tile_cols`: among one device's live tiles at most 8 have their row block held by any one device of that row group, and at most 4 have their column block held by any one device of that column group.
All inputs are finite; a program needn't handle non-finite values.
Results may differ from the reference program's by a relative error of at most 0.013.
Values may be sent and summed in bfloat16 or wider, within the bound.
No kernel may reach another device: no remote copies, remote signals or barrier semaphores. Data moves between devices by JAX's collectives and lax.ppermute only.
A program may use at most 128 MiB of HBM per device.

```python
import math
import jax
import jax.numpy as jnp
from jax import lax

D = 512
BS = 128
BLK_DEV = 4
KMAX = 64
BLOCKS = 512
ATOMS = 65536
N_ROW = 16
N_COL = 8


def slot_order(sub_key):
    return jax.random.permutation(sub_key, KMAX)


def tile_layout(key):
    base_key = jax.random.fold_in(key, 4711)
    key_list = jax.random.split(base_key, 5)
    device_total = N_ROW * N_COL
    full_device = jax.random.randint(key_list[0], (), 0, device_total)
    partial_counts = jax.random.randint(key_list[1], (device_total,), KMAX // 4, 3 * KMAX // 4 + 1)
    counts = jnp.where(jnp.arange(device_total) == full_device, KMAX, partial_counts).astype(jnp.int32)
    orders = jax.vmap(slot_order)(jax.random.split(key_list[2], device_total)).astype(jnp.int32)
    row_owner = orders % N_ROW
    col_owner = (orders // N_ROW + orders) % N_COL
    device_ids = jnp.arange(device_total, dtype=jnp.int32)
    device_rows = (device_ids // N_COL)[:, None]
    device_cols = (device_ids % N_COL)[:, None]
    row_pick = jax.random.randint(key_list[3], (device_total, KMAX), 0, BLK_DEV)
    col_pick = jax.random.randint(key_list[4], (device_total, KMAX), 0, BLK_DEV)
    rows = device_rows * (BLK_DEV * N_COL) + col_owner * BLK_DEV + row_pick
    cols = row_owner * (BLK_DEV * N_COL) + device_cols * BLK_DEV + col_pick
    return (rows.reshape(N_ROW, N_COL, KMAX).astype(jnp.int32), cols.reshape(N_ROW, N_COL, KMAX).astype(jnp.int32), counts.reshape(N_ROW, N_COL))


def draw_tile_rows(key, part):
    return tile_layout(key)[0]


def draw_tile_cols(key, part):
    return tile_layout(key)[1]


def draw_tile_counts(key, part):
    return tile_layout(key)[2]


def shard_levels(stream_key, dims, pieces, low, top_value):
    factor_of, own = 1.0, jax.random.fold_in(stream_key, 6)
    for dim, blocks in pieces:
        draws = jnp.exp(jax.random.uniform(jax.random.fold_in(own, dim), (blocks,), jnp.float32, low / len(pieces), top_value / len(pieces)))
        factor_of = factor_of * jnp.repeat(draws, dims[dim] // blocks).reshape([-1 if axis == dim else 1 for axis in range(len(dims))])
    return factor_of


def scatter_about(key, extent, scale, reach, cuts=(), kind=jnp.bfloat16):
    loudness = shard_levels(key, extent, cuts, -0.22, 0.18) if cuts else 1.0
    drawn = jax.random.normal(key, extent, jnp.float32) * scale * loudness
    return jnp.minimum(jnp.maximum(drawn, -reach), reach).astype(kind)


def setup_inputs(seed: int = 0) -> dict:
    keys = jax.random.split(jax.random.key(seed), 9)
    features = scatter_about(keys[0], (ATOMS, D), 1.0, 6.0, ((0, 128),))
    weight = scatter_about(keys[1], (D, D), D ** -0.5, 0.25)
    bias = scatter_about(keys[2], (D,), 0.5, 3.0, (), jnp.float32)
    cotangent = scatter_about(keys[3], (ATOMS, D), 1.0, 6.0, ((0, 128),))
    tile_values = scatter_about(keys[4], (N_ROW, N_COL, KMAX, BS, BS), (8 * BS) ** -0.5, 0.1875, ((0, 16), (1, 8)))
    tile_rows = draw_tile_rows(jax.random.fold_in(keys[8], 71), 0)
    tile_cols = draw_tile_cols(jax.random.fold_in(keys[8], 71), 0)
    tile_counts = draw_tile_counts(jax.random.fold_in(keys[8], 71), 0)
    return dict(features=features, weight=weight, bias=bias, cotangent=cotangent, tile_values=tile_values, tile_rows=tile_rows, tile_cols=tile_cols, tile_counts=tile_counts)


def block_products(tiles, alive, source_blocks, fetch_ids, add_ids, transpose):

    def step(carry, items):
        tile_group, fetch_row, add_row, alive_row = items
        picked = source_blocks[fetch_row].astype(jnp.float32)
        mats = tile_group.astype(jnp.float32)
        if transpose:
            products = jnp.einsum('kba,kbd->kad', mats, picked)
        else:
            products = jnp.einsum('kab,kbd->kad', mats, picked)
        products = products * alive_row.astype(jnp.float32)[:, None, None]
        return (carry.at[add_row].add(products), None)
    initial = jnp.zeros((BLOCKS, BS, D), jnp.float32)
    total, unused = lax.scan(step, initial, (tiles, fetch_ids, add_ids, alive))
    return total.reshape(ATOMS, D)

def reference(features, weight, bias, cotangent, tile_values, tile_rows, tile_cols, tile_counts):
    device_total = N_ROW * N_COL
    tiles = tile_values.reshape(device_total, KMAX, BS, BS)
    row_ids = tile_rows.reshape(device_total, KMAX).astype(jnp.int32)
    col_ids = tile_cols.reshape(device_total, KMAX).astype(jnp.int32)
    alive = jnp.arange(KMAX, dtype=jnp.int32)[None, :] < tile_counts.reshape(device_total, 1)
    feature_blocks = features.reshape(BLOCKS, BS, D)
    aggregated = block_products(tiles, alive, feature_blocks, col_ids, row_ids, False).astype(jnp.bfloat16)
    pre_act = jnp.dot(aggregated, weight, preferred_element_type=jnp.float32) + bias.astype(jnp.float32)
    sigm = jax.nn.sigmoid(pre_act)
    output = (pre_act * sigm).astype(jnp.bfloat16)
    grad_pre = (cotangent.astype(jnp.float32) * sigm * (1.0 + pre_act * (1.0 - sigm))).astype(jnp.bfloat16)
    scale = 1.0 / math.sqrt(ATOMS)
    weight_grad = jnp.dot(aggregated.T, grad_pre, preferred_element_type=jnp.float32) * scale
    bias_grad = lax.optimization_barrier(jnp.sum(grad_pre.astype(jnp.float32), axis=0)) * scale
    grad_agg = jnp.dot(grad_pre, weight.T, preferred_element_type=jnp.float32).astype(jnp.bfloat16)
    grad_blocks = grad_agg.reshape(BLOCKS, BS, D)
    feature_grad = block_products(tiles, alive, grad_blocks, row_ids, col_ids, True).astype(jnp.bfloat16)
    return (output, feature_grad, weight_grad, bias_grad)
```

```python
import functools
import math

import jax
import jax.numpy as jnp
from jax import lax
from jax.experimental import pallas as pl
from jax.experimental.pallas import tpu as pltpu
from jax.sharding import PartitionSpec as P

BF = jnp.bfloat16
F32 = jnp.float32
X = 4
VMEM_LIMIT = 56 * 2**20
UNROLL = 4


def tile_loop(count, step):
    def body(i, carry):
        for j in range(UNROLL):
            k = i * UNROLL + j
            step(k, k < count)
        return carry

    lax.fori_loop(0, (count + UNROLL - 1) // UNROLL, body, 0)


def zero(acc, blocks):
    def body(i, carry):
        acc[i] = jnp.zeros(acc.shape[1:], acc.dtype)
        return carry

    lax.fori_loop(0, blocks, body, 0)


def forward_kernel(cols, rows, count, tiles, near, far, out, source, vals, acc, sems):
    core = lax.axis_index("row") % 2
    copies = [
        pltpu.make_async_copy(near, source.at[0], sems.at[0]),
        pltpu.make_async_copy(far, source.at[1], sems.at[1]),
        pltpu.make_async_copy(tiles, vals, sems.at[2]),
    ]
    for copy in copies:
        copy.start()
    blocks = acc.shape[0] - 1
    zero(acc, blocks)
    for copy in copies:
        copy.wait()

    def step(k, live):
        col = cols[k]
        owner = col // 32
        far_core = lax.rem(lax.rem(owner, 2) + core, 2)
        place = owner // 2 * 4 + lax.rem(col, 4)
        target = jnp.where(live, lax.rem(rows[k], blocks), blocks)
        acc[target] += jnp.dot(vals[k], source[far_core, place], preferred_element_type=F32)

    tile_loop(count[0], step)

    def store(i, carry):
        out[i] = acc[i].astype(BF)
        return carry

    lax.fori_loop(0, blocks, store, 0)


def backward_kernel(cols, rows, count, tiles, spread, far_out, near_out, weight_out, source, shares, vals, acc, sems):
    node_dev = spread.shape[2] * 4
    me = lax.axis_index("row")
    core = me % 2
    my_y = me // 8
    my_x = me // 2 % X
    members = spread.shape[0]
    copies = [
        pltpu.make_async_copy(spread.at[:, pl.ds(0, 512)], source, sems.at[0]),
        pltpu.make_async_copy(spread.at[:, pl.ds(512, 80)], shares, sems.at[1]),
        pltpu.make_async_copy(tiles, vals, sems.at[2]),
    ]
    for copy in copies:
        copy.start()
    blocks = acc.shape[0] - 1
    zero(acc, blocks)
    for copy in copies:
        copy.wait()
    total = shares[0].astype(F32)
    for j in range(1, members):
        total += shares[j].astype(F32)
    weight_out[...] = total

    def step(k, live):
        col = cols[k]
        owner = col // 32
        far_core = lax.rem(owner % 2 + core, 2)
        far_y = lax.rem(owner // 8 + my_y, 2)
        far_x = lax.rem(owner // 2 % X + X - my_x, X)
        target = far_core * 32 + far_y * 16 + far_x * 4 + lax.rem(col, 4)
        target = jnp.where(live, target, blocks)
        row = lax.rem(rows[k], 32)
        start = pl.multiple_of(lax.rem(row, 4) * 128, 128)
        picked = source[row // 4, pl.ds(start, 128), :]
        acc[target] += lax.dot_general(
            vals[k], picked, (((0,), (0,)), ((), ())), preferred_element_type=F32
        )

    tile_loop(count[0], step)

    def store(i, carry):
        near_out[i] = acc[i].astype(BF)
        far_out[i] = acc[i + 32].astype(BF)
        return carry

    lax.fori_loop(0, 32, store, 0)


def dense_kernel(scale, parts, weight, bias, cotangent, output, spread, agg, grad_pre):
    members = parts.shape[0]
    size = 128

    def body(i, bias_sum):
        at = pl.ds(pl.multiple_of(i * size, size), size)
        total = parts[0, at, :].astype(F32)
        for j in range(1, members):
            total += parts[j, at, :].astype(F32)
        value = total.astype(BF)
        agg[at, :] = value
        pre = jnp.dot(value, weight[...], preferred_element_type=F32) + bias[...]
        s = jax.nn.sigmoid(pre)
        output[at, :] = (pre * s).astype(BF)
        grad = (cotangent[at, :].astype(F32) * s * (1.0 + pre * (1.0 - s))).astype(BF)
        grad_pre[at, :] = grad
        back = lax.dot_general(grad, weight[...], (((1,), (1,)), ((), ())), preferred_element_type=F32).astype(BF)
        for j in range(members):
            spread[j, at, :] = back
        return bias_sum + jnp.sum(grad.astype(F32), axis=0, keepdims=True)

    bias_sum = lax.fori_loop(0, agg.shape[0] // size, body, jnp.zeros((1, agg.shape[1]), F32))
    share = agg.shape[1] // members
    bias_high = (bias_sum * scale).astype(BF).astype(F32)
    bias_low = bias_sum * scale - bias_high
    row = lax.broadcasted_iota(jnp.int32, (16, agg.shape[1]), 0)
    tail = jnp.where(row == 0, bias_high, jnp.where(row == 1, bias_low, 0.0)).astype(BF)
    weight_part = lax.dot_general(agg[...], grad_pre[...], (((0,), (0,)), ((), ())), preferred_element_type=F32)
    for j in range(members):
        spread[j, pl.ds(512, share), :] = (weight_part[j * share : (j + 1) * share] * scale).astype(BF)
        spread[j, pl.ds(512 + share, 16), :] = tail


def any_spec():
    return pl.BlockSpec(memory_space=pl.ANY)


def vmem_spec():
    return pl.BlockSpec(memory_space=pltpu.VMEM)


def call(kernel, ids, args, in_specs, out_shape, scratch, flops, moved):
    shapes = [jax.ShapeDtypeStruct(s, d) for s, d in out_shape]
    return pl.pallas_call(
        kernel,
        grid_spec=pltpu.PrefetchScalarGridSpec(
            num_scalar_prefetch=len(ids),
            in_specs=in_specs,
            out_specs=[vmem_spec() for _ in shapes],
            scratch_shapes=scratch,
        ),
        out_shape=shapes,
        compiler_params=pltpu.CompilerParams(vmem_limit_bytes=VMEM_LIMIT),
        cost_estimate=pl.CostEstimate(flops=flops, bytes_accessed=moved, transcendentals=0),
    )(*ids, *args)


def core_swap(value):
    return lax.ppermute(value, "row", [(i, i ^ 1) for i in range(16)])


def row_shift(value, dy, dx):
    def to(i):
        y, x, core = i // 8, i // 2 % X, i % 2
        return (y ^ dy) * 8 + (x + dx) % X * 2 + core

    return lax.ppermute(value, "row", [(i, to(i)) for i in range(16)])


def on_device(features, weight, bias, cotangent, tile_values, tile_rows, tile_cols, tile_counts):
    same_core = [[i for i in range(16) if i % 2 == c] for c in range(2)]
    tiles = tile_values.reshape(64, 128, 128)
    cols = tile_cols.reshape(64)
    rows = tile_rows.reshape(64)
    count = tile_counts.reshape(1)
    scale = 1.0 / math.sqrt(65536)

    near = lax.all_to_all(
        jnp.broadcast_to(features[None], (8, 512, 512)), "row", 0, 0, tiled=True, axis_index_groups=same_core
    )
    far = core_swap(near)
    (partial,) = call(
        forward_kernel,
        (cols, rows, count),
        (tiles, near.reshape(32, 128, 512), far.reshape(32, 128, 512)),
        [any_spec()] * 3,
        [((32, 128, 512), BF)],
        [
            pltpu.VMEM((2, 32, 128, 512), BF),
            pltpu.VMEM((64, 128, 128), BF),
            pltpu.VMEM((33, 128, 512), F32),
            pltpu.SemaphoreType.DMA((3,)),
        ],
        2 * 64 * 128 * 128 * 512,
        14 * 2**20,
    )
    parts = lax.all_to_all(partial.reshape(8, 512, 512), "col", 0, 0, tiled=True)
    output, spread = call(
        functools.partial(dense_kernel, scale),
        (),
        (parts, weight, bias.reshape(1, 512), cotangent),
        [vmem_spec()] * 4,
        [((512, 512), BF), ((8, 592, 512), BF)],
        [pltpu.VMEM((512, 512), BF), pltpu.VMEM((512, 512), BF)],
        6 * 512**3,
        10 * 2**20,
    )
    spread = lax.all_to_all(spread, "col", 0, 0, tiled=True)
    far_part, near_part, share = call(
        backward_kernel,
        (cols, rows, count),
        (tiles, spread),
        [any_spec()] * 2,
        [((32, 128, 512), BF), ((32, 128, 512), BF), ((80, 512), F32)],
        [
            pltpu.VMEM((8, 512, 512), BF),
            pltpu.VMEM((8, 80, 512), BF),
            pltpu.VMEM((64, 128, 128), BF),
            pltpu.VMEM((65, 128, 512), F32),
            pltpu.SemaphoreType.DMA((3,)),
        ],
        2 * 64 * 128 * 128 * 512,
        14 * 2**20,
    )
    far_part = core_swap(far_part).reshape(8, 512, 512)
    near_part = near_part.reshape(8, 512, 512)
    sums = [near_part[i].astype(F32) + far_part[i].astype(F32) for i in range(8)]
    total = sums[0]
    for i in range(1, 8):
        total = total + row_shift(sums[i].astype(BF), i // X, i % X).astype(F32)
    feature_grad = total.astype(BF)

    bias_share = (share[64:65] + share[65:66]).reshape(1, 1, 512)
    weight_share = share[:64].reshape(16, 4, 512)
    pieces = jnp.concatenate(
        [weight_share, jnp.broadcast_to(bias_share, (16, 1, 512)), jnp.zeros((16, 3, 512), F32)], axis=1
    )
    pieces = jnp.sum(lax.all_to_all(pieces, "row", 0, 0, tiled=True), axis=0)
    bias_grad = pieces[4]
    own = lax.all_to_all(jnp.broadcast_to(pieces[None, :4], (16, 4, 512)), "row", 0, 0, tiled=True)
    whole = lax.all_to_all(jnp.broadcast_to(own.reshape(1, 64, 512), (8, 64, 512)), "col", 0, 0, tiled=True)
    weight_grad = whole.reshape(512, 512)
    return (output, feature_grad, weight_grad, bias_grad)


def solution(mesh):
    return jax.shard_map(
        on_device,
        mesh=mesh,
        in_specs=(
            P(("row", "col"), None),
            P(),
            P(),
            P(("row", "col"), None),
            P("row", "col", None, None, None),
            P("row", "col", None),
            P("row", "col", None),
            P("row", "col"),
        ),
        out_specs=(P(("row", "col"), None), P(("row", "col"), None), P(), P()),
        check_vma=False,
    )
```

```python
import functools
import math

import jax
import jax.numpy as jnp
from jax import lax
from jax.experimental import pallas as pl
from jax.experimental.pallas import tpu as pltpu
from jax.sharding import PartitionSpec as P

BF = jnp.bfloat16
F32 = jnp.float32
VMEM_LIMIT = 56 * 2**20
UNROLL = 16
HALF = 256
SHARE = 32
TAIL = 16
LINES = [[(chip * 2 + core) * 8 + q for core in range(2) for q in range(8)] for chip in range(8)]


def tile_loop(count, acc, step):
    def body(i, carry):
        found = [step(i * UNROLL + j, i * UNROLL + j < count) for j in range(UNROLL)]
        for target, product in found:
            acc[target] += product
        return carry

    lax.fori_loop(0, (count + UNROLL - 1) // UNROLL, body, 0)


def loop(n, step):
    def body(i, carry):
        step(i)
        return carry

    lax.fori_loop(0, n, body, 0)


def start_loads(sources, acc, sems):
    copies = [pltpu.make_async_copy(a, b, sems.at[i]) for i, (a, b) in enumerate(sources)]
    for copy in copies:
        copy.start()

    @functools.partial(loop, acc.shape[0] - 1)
    def _(i):
        acc[i] = jnp.zeros(acc.shape[1:], F32)

    for copy in copies:
        copy.wait()


def copies_kernel(features, out, sems):
    copies = [
        pltpu.make_async_copy(features.at[:, pl.ds(j % 2 * HALF, HALF)], out.at[j], sems.at[j]) for j in range(16)
    ]
    for copy in copies:
        copy.start()
    for copy in copies:
        copy.wait()


def forward_kernel(ids, other_ids, tiles, other_tiles, gathered, out, source, vals, acc, sems):
    core = lax.axis_index("row") % 2
    start_loads([(tiles, vals.at[0]), (other_tiles, vals.at[1]), (gathered, source)], acc, sems)
    for side, table in enumerate((ids, other_ids)):
        group = core if side == 0 else 1 - core

        @functools.partial(tile_loop, table[128], acc)
        def _(k, live, side=side, table=table, group=group):
            col, row = table[k], table[64 + k]
            start = pl.multiple_of(lax.rem(col, 4) * 128, 128)
            picked = source[col // 32, pl.ds(start, 128), :]
            target = jnp.where(live, group * 32 + lax.rem(row, 32), 64)
            return target, jnp.dot(vals[side, k], picked, preferred_element_type=F32)

    @functools.partial(loop, 64)
    def _(i):
        out[i] = acc[i].astype(BF)


def backward_kernel(ids, other_ids, tiles, other_tiles, spread, out, source, vals, acc, sems):
    core = lax.axis_index("row") % 2
    start_loads(
        [(tiles, vals.at[0]), (other_tiles, vals.at[1]), (spread, source)], acc, sems
    )
    for side, table in enumerate((ids, other_ids)):
        group = core if side == 0 else 1 - core

        @functools.partial(tile_loop, table[128], acc)
        def _(k, live, side=side, table=table, group=group):
            col, row = table[k], lax.rem(table[64 + k], 32)
            start = pl.multiple_of(lax.rem(row, 4) * 128, 128)
            picked = source[group * 8 + row // 4, pl.ds(start, 128), :]
            target = jnp.where(live, col // 32 * 4 + lax.rem(col, 4), 64)
            return target, lax.dot_general(
                vals[side, k], picked, (((0,), (0,)), ((), ())), preferred_element_type=F32
            )

    @functools.partial(loop, 64)
    def _(i):
        out[i] = acc[i].astype(BF)


def row_place():
    me = lax.axis_index("row")
    return lax.rem(me // 2, 4), lax.rem(me, 2)


def dense_kernel(scale, parts, weight, bias, cotangent, output, spread, chunks, agg, grad_pre, product):
    size = 128

    def body(i, bias_sum):
        at = pl.ds(pl.multiple_of(i * size, size), size)
        for half in range(2):
            total = parts[half * 8, at, :].astype(F32)
            for j in range(1, 8):
                total += parts[half * 8 + j, at, :].astype(F32)
            agg[at, half * HALF : (half + 1) * HALF] = total.astype(BF)
        pre = jnp.dot(agg[at, :], weight[...], preferred_element_type=F32) + bias[...]
        s = jax.nn.sigmoid(pre)
        output[at, :] = (pre * s).astype(BF)
        grad = (cotangent[at, :].astype(F32) * s * (1.0 + pre * (1.0 - s))).astype(BF)
        grad_pre[at, :] = grad
        back = lax.dot_general(grad, weight[...], (((1,), (1,)), ((), ())), preferred_element_type=F32).astype(BF)
        for j in range(16):
            spread[j, at, :] = back[:, j // 8 * HALF : (j // 8 + 1) * HALF]
        return bias_sum + jnp.sum(grad.astype(F32), axis=0, keepdims=True)

    bias_sum = lax.fori_loop(0, agg.shape[0] // size, body, jnp.zeros((1, agg.shape[1]), F32)) * scale
    product[...] = lax.dot_general(agg[...], grad_pre[...], (((0,), (0,)), ((), ())), preferred_element_type=F32)
    tail = jnp.broadcast_to(bias_sum, (TAIL, agg.shape[1])).astype(BF)
    my_x, my_core = row_place()
    for core in range(2):
        for x in range(4):
            for y in range(2):
                owner = y * 8 + lax.rem(my_x + x, 4) * 2 + lax.rem(my_core + core, 2)
                rows = product[pl.ds(pl.multiple_of(owner * SHARE, SHARE), SHARE), :]
                chunks[core, x, y, :SHARE, :] = (rows * scale).astype(BF)
                chunks[core, x, y, SHARE:, :] = tail


def place_kernel(own, moved_1, moved_2, moved_3, weight_grad, bias_grad):
    my_x, my_core = row_place()
    my_z = lax.axis_index("col") // 2
    for d, piece in enumerate((own, moved_1, moved_2, moved_3)):
        for j in range(4):
            flat = lax.rem(my_z + 4 - d, 4) * 4 + j
            core, x, y = flat // 8, lax.rem(flat // 2, 4), j % 2
            owner = y * 8 + lax.rem(my_x + 4 - x, 4) * 2 + lax.rem(my_core + core, 2)
            at = pl.ds(pl.multiple_of(owner * SHARE, SHARE), SHARE)
            weight_grad[at, :] = piece[j, :SHARE, :].astype(F32)
    bias_grad[...] = own[0, SHARE : SHARE + 1, :].astype(F32)


def final_kernel(parts, out):
    @functools.partial(loop, 4)
    def _(i):
        at = pl.ds(pl.multiple_of(i * 128, 128), 128)
        for half in range(2):
            total = parts[half, at, :].astype(F32)
            for j in range(1, 8):
                total += parts[2 * j + half, at, :].astype(F32)
            out[at, half * HALF : (half + 1) * HALF] = total.astype(BF)


def any_spec():
    return pl.BlockSpec(memory_space=pl.ANY)


def vmem_spec():
    return pl.BlockSpec(memory_space=pltpu.VMEM)


def call(kernel, args, out_shape, ids=(), in_specs=None, out_specs=None, scratch=(), flops=0, moved=4 * 2**20):
    shapes = [jax.ShapeDtypeStruct(s, d) for s, d in out_shape]
    return pl.pallas_call(
        kernel,
        grid_spec=pltpu.PrefetchScalarGridSpec(
            num_scalar_prefetch=len(ids),
            in_specs=in_specs or [vmem_spec() for _ in args],
            out_specs=out_specs or [vmem_spec() for _ in shapes],
            scratch_shapes=scratch,
        ),
        out_shape=shapes,
        compiler_params=pltpu.CompilerParams(vmem_limit_bytes=VMEM_LIMIT),
        cost_estimate=pl.CostEstimate(flops=flops, bytes_accessed=moved, transcendentals=0),
    )(*ids, *args)


def core_swap(value):
    return lax.ppermute(value, "row", [(i, i ^ 1) for i in range(16)])


def swap_y(value, high, low):
    to = [(i, i ^ (64 * high + low)) for i in range(128)]
    return lax.ppermute(value, ("row", "col"), to)


def shift(value, axis, d):
    if axis == "row":
        to = [(i, i // 8 * 8 + (i + 2 * d) % 8) for i in range(16)]
    else:
        to = [(i, (i + 2 * d) % 8) for i in range(8)]
    return lax.ppermute(value, axis, to)


def add(*parts):
    total = parts[0].astype(F32)
    for part in parts[1:]:
        total = total + part.astype(F32)
    return total.astype(BF)


def plane_sum(chunks):
    part = add(chunks[0], core_swap(chunks[1]))
    part = add(part[0], *(shift(part[d], "row", d) for d in range(1, 4)))
    return add(part, swap_y(part, 0, 1), swap_y(part, 1, 0), swap_y(part, 1, 1))


def ring(part, axis):
    return (part, *(shift(part, axis, d) for d in range(1, 4)))


def z_sum(chunks):
    z = lax.axis_index("col") // 2
    parts = chunks.reshape(4, 4, *chunks.shape[-2:])

    def part_of(d):
        return lax.dynamic_index_in_dim(parts, (z + d) % 4, 0, keepdims=False)

    return ring(add(part_of(0), *(shift(part_of(d), "col", d) for d in range(1, 4))), "col")


def row_exchange(value):
    return lax.all_to_all(value, "row", 0, 0, tiled=True)


def line_exchange(value):
    return lax.all_to_all(value, ("row", "col"), 0, 0, tiled=True, axis_index_groups=LINES)


def on_device(features, weight, bias, cotangent, tile_values, tile_rows, tile_cols, tile_counts):
    tiles = tile_values.reshape(64, 128, 128)
    ids = jnp.concatenate([tile_cols.reshape(64), tile_rows.reshape(64), tile_counts.reshape(1)])
    other_tiles, other_ids = core_swap(tiles), core_swap(ids)
    scale = 1.0 / math.sqrt(65536)
    tables = (ids, other_ids)
    scratch = [
        pltpu.VMEM((16, 512, HALF), BF),
        pltpu.VMEM((2, 64, 128, 128), BF),
        pltpu.VMEM((65, 128, HALF), F32),
        pltpu.SemaphoreType.DMA((3,)),
    ]
    work = dict(
        ids=tables, in_specs=[any_spec()] * 3, scratch=scratch, flops=2 * 64 * 128 * 128 * 512, moved=16 * 2**20
    )

    (copies,) = call(
        copies_kernel,
        (features,),
        [((16, 512, HALF), BF)],
        out_specs=[any_spec()],
        scratch=[pltpu.SemaphoreType.DMA((16,))],
    )
    gathered = row_exchange(copies)
    (partial,) = call(forward_kernel, (tiles, other_tiles, gathered), [((64, 128, HALF), BF)], **work)
    parts = line_exchange(partial.reshape(16, 512, HALF))
    output, spread, chunks = call(
        functools.partial(dense_kernel, scale),
        (parts, weight, bias.reshape(1, 512), cotangent),
        [((512, 512), BF), ((16, 512, HALF), BF), ((2, 4, 2, SHARE + TAIL, 512), BF)],
        scratch=[pltpu.VMEM((512, 512), BF), pltpu.VMEM((512, 512), BF), pltpu.VMEM((512, 512), F32)],
        flops=6 * 512**3,
        moved=8 * 2**20,
    )
    spread = line_exchange(spread)
    chunks, spread = lax.optimization_barrier((plane_sum(chunks), spread))
    (back,) = call(backward_kernel, (tiles, other_tiles, spread), [((64, 128, HALF), BF)], **work)
    chunks, back = lax.optimization_barrier((jnp.stack(ring(chunks, "row")), back))
    back = row_exchange(back.reshape(16, 512, HALF))
    chunks = jnp.stack([chunks, core_swap(chunks)])
    weight_grad, bias_grad = call(place_kernel, z_sum(chunks), [((512, 512), F32), ((1, 512), F32)])
    (feature_grad,) = call(final_kernel, (back,), [((512, 512), BF)])
    return (output, feature_grad, weight_grad, bias_grad.reshape(512))


def solution(mesh):
    return jax.shard_map(
        on_device,
        mesh=mesh,
        in_specs=(
            P(("row", "col"), None),
            P(),
            P(),
            P(("row", "col"), None),
            P("row", "col", None, None, None),
            P("row", "col", None),
            P("row", "col", None),
            P("row", "col"),
        ),
        out_specs=(P(("row", "col"), None), P(("row", "col"), None), P(), P()),
        check_vma=False,
    )
```

```python
import functools
import math

import jax
import jax.numpy as jnp
from jax import lax
from jax.experimental import pallas as pl
from jax.experimental.pallas import tpu as pltpu
from jax.sharding import PartitionSpec as P

BF = jnp.bfloat16
F32 = jnp.float32
VMEM_LIMIT = 26 * 2**20
UNROLL = 16
HALF = 256
FIRST = 256
SHARE = 32
TAIL = 16
LINES = [[(chip * 2 + core) * 8 + q for core in range(2) for q in range(8)] for chip in range(8)]


def tile_loop(count, acc, step):
    def body(i, carry):
        found = [step(i * UNROLL + j, i * UNROLL + j < count) for j in range(UNROLL)]
        for target, product in found:
            acc[target] += product
        return carry

    lax.fori_loop(0, (count + UNROLL - 1) // UNROLL, body, 0)


def loop(n, step):
    def body(i, carry):
        step(i)
        return carry

    lax.fori_loop(0, n, body, 0)


def start_loads(sources, acc, sems):
    copies = [pltpu.make_async_copy(a, b, sems.at[i]) for i, (a, b) in enumerate(sources)]
    for copy in copies:
        copy.start()

    @functools.partial(loop, acc.shape[0] - 1)
    def _(i):
        acc[i] = jnp.zeros(acc.shape[1:], F32)

    for copy in copies:
        copy.wait()


def halves_kernel(features, mine, other):
    left = lax.axis_index("row") % 2 == 0
    first, second = features[:, :HALF], features[:, HALF:]
    mine[...] = jnp.where(left, first, second)
    other[...] = jnp.where(left, second, first)


def route_loads(pieces, source):
    own, ring_1, ring_2, ring_3, near, far = pieces
    low, high = pl.ds(0, FIRST), pl.ds(FIRST, 512 - FIRST)
    loads = [(piece, source.at[d, :, :, low]) for d, piece in enumerate((own, ring_1, ring_2, ring_3))]
    return loads + [(near, source.at[:, 0, :, high]), (far, source.at[:, 1, :, high])]


def forward_kernel(ids, other_ids, tiles, other_tiles, *refs):
    *pieces, out, source, vals, acc, sems = refs
    me = lax.axis_index("row")
    core, my_x, my_y = lax.rem(me, 2), lax.rem(me // 2, 4), me // 8
    start_loads([(tiles, vals.at[0]), (other_tiles, vals.at[1]), *route_loads(pieces, source)], acc, sems)
    for side, table in enumerate((ids, other_ids)):
        group = core if side == 0 else 1 - core

        @functools.partial(tile_loop, table[128], acc)
        def _(k, live, side=side, table=table, group=group):
            col, row = table[k], table[64 + k]
            start = pl.multiple_of(lax.rem(col, 4) * 128, 128)
            owner = col // 32
            behind = lax.rem(my_x + 4 - lax.rem(owner // 2, 4), 4)
            y, far_core = lax.rem(owner // 8 + my_y, 2), lax.rem(owner + core, 2)
            picked = source[behind, y, far_core, pl.ds(start, 128), :]
            target = jnp.where(live, group * 32 + lax.rem(row, 32), 64)
            return target, jnp.dot(vals[side, k], picked, preferred_element_type=F32)

    @functools.partial(loop, 64)
    def _(i):
        out[i] = acc[i].astype(BF)


def backward_kernel(ids, other_ids, tiles, other_tiles, spread, out, source, vals, acc, sems):
    core = lax.axis_index("row") % 2
    start_loads(
        [(tiles, vals.at[0]), (other_tiles, vals.at[1]), (spread, source)], acc, sems
    )
    for side, table in enumerate((ids, other_ids)):
        group = core if side == 0 else 1 - core

        @functools.partial(tile_loop, table[128], acc)
        def _(k, live, side=side, table=table, group=group):
            col, row = table[k], lax.rem(table[64 + k], 32)
            start = pl.multiple_of(lax.rem(row, 4) * 128, 128)
            picked = source[group * 8 + row // 4, pl.ds(start, 128), :]
            target = jnp.where(live, col // 32 * 4 + lax.rem(col, 4), 64)
            return target, lax.dot_general(
                vals[side, k], picked, (((0,), (0,)), ((), ())), preferred_element_type=F32
            )

    @functools.partial(loop, 64)
    def _(i):
        out[i] = acc[i].astype(BF)


def row_place():
    me = lax.axis_index("row")
    return lax.rem(me // 2, 4), lax.rem(me, 2)


def dense_kernel(scale, parts, weight, bias, cotangent, output, spread, chunks, agg, grad_pre, product):
    size = 128

    def body(i, bias_sum):
        at = pl.ds(pl.multiple_of(i * size, size), size)
        for half in range(2):
            total = parts[half * 8, at, :].astype(F32)
            for j in range(1, 8):
                total += parts[half * 8 + j, at, :].astype(F32)
            agg[at, half * HALF : (half + 1) * HALF] = total.astype(BF)
        pre = jnp.dot(agg[at, :], weight[...], preferred_element_type=F32) + bias[...]
        s = jax.nn.sigmoid(pre)
        output[at, :] = (pre * s).astype(BF)
        grad = (cotangent[at, :].astype(F32) * s * (1.0 + pre * (1.0 - s))).astype(BF)
        grad_pre[at, :] = grad
        back = lax.dot_general(grad, weight[...], (((1,), (1,)), ((), ())), preferred_element_type=F32).astype(BF)
        for j in range(16):
            spread[j, at, :] = back[:, j // 8 * HALF : (j // 8 + 1) * HALF]
        return bias_sum + jnp.sum(grad.astype(F32), axis=0, keepdims=True)

    bias_sum = lax.fori_loop(0, agg.shape[0] // size, body, jnp.zeros((1, agg.shape[1]), F32)) * scale
    product[...] = lax.dot_general(agg[...], grad_pre[...], (((0,), (0,)), ((), ())), preferred_element_type=F32)
    tail = jnp.broadcast_to(bias_sum, (TAIL, agg.shape[1])).astype(BF)
    my_x, my_core = row_place()
    for core in range(2):
        for x in range(4):
            for y in range(2):
                owner = y * 8 + lax.rem(my_x + x, 4) * 2 + lax.rem(my_core + core, 2)
                rows = product[pl.ds(pl.multiple_of(owner * SHARE, SHARE), SHARE), :]
                chunks[core, x, y, :SHARE, :] = (rows * scale).astype(BF)
                chunks[core, x, y, SHARE:, :] = tail


def place_kernel(own, moved_1, moved_2, moved_3, weight_grad, bias_grad):
    my_x, my_core = row_place()
    my_z = lax.axis_index("col") // 2
    for d, piece in enumerate((own, moved_1, moved_2, moved_3)):
        for j in range(4):
            flat = lax.rem(my_z + 4 - d, 4) * 4 + j
            core, x, y = flat // 8, lax.rem(flat // 2, 4), j % 2
            owner = y * 8 + lax.rem(my_x + 4 - x, 4) * 2 + lax.rem(my_core + core, 2)
            at = pl.ds(pl.multiple_of(owner * SHARE, SHARE), SHARE)
            weight_grad[at, :] = piece[j, :SHARE, :].astype(F32)
    bias_grad[...] = own[0, SHARE : SHARE + 1, :].astype(F32)


def final_kernel(parts, out):
    @functools.partial(loop, 4)
    def _(i):
        at = pl.ds(pl.multiple_of(i * 128, 128), 128)
        for half in range(2):
            total = parts[half, at, :].astype(F32)
            for j in range(1, 8):
                total += parts[2 * j + half, at, :].astype(F32)
            out[at, half * HALF : (half + 1) * HALF] = total.astype(BF)


def any_spec():
    return pl.BlockSpec(memory_space=pl.ANY)


def vmem_spec():
    return pl.BlockSpec(memory_space=pltpu.VMEM)


def call(kernel, args, out_shape, ids=(), in_specs=None, out_specs=None, scratch=(), flops=0, moved=4 * 2**20):
    shapes = [jax.ShapeDtypeStruct(s, d) for s, d in out_shape]
    return pl.pallas_call(
        kernel,
        grid_spec=pltpu.PrefetchScalarGridSpec(
            num_scalar_prefetch=len(ids),
            in_specs=in_specs or [vmem_spec() for _ in args],
            out_specs=out_specs or [vmem_spec() for _ in shapes],
            scratch_shapes=scratch,
        ),
        out_shape=shapes,
        compiler_params=pltpu.CompilerParams(vmem_limit_bytes=VMEM_LIMIT),
        cost_estimate=pl.CostEstimate(flops=flops, bytes_accessed=moved, transcendentals=0),
    )(*ids, *args)


def core_swap(value):
    return lax.ppermute(value, "row", [(i, i ^ 1) for i in range(16)])


def swap_y(value, high, low):
    to = [(i, i ^ (64 * high + low)) for i in range(128)]
    return lax.ppermute(value, ("row", "col"), to)


def shift(value, axis, d):
    if axis == "row":
        to = [(i, i // 8 * 8 + (i + 2 * d) % 8) for i in range(16)]
    else:
        to = [(i, (i + 2 * d) % 8) for i in range(8)]
    return lax.ppermute(value, axis, to)


def add(*parts):
    total = parts[0].astype(F32)
    for part in parts[1:]:
        total = total + part.astype(F32)
    return total.astype(BF)


def plane_sum(chunks):
    part = add(chunks[0], core_swap(chunks[1]))
    part = add(part[0], *(shift(part[d], "row", d) for d in range(1, 4)))
    return add(part, swap_y(part, 0, 1), swap_y(part, 1, 0), swap_y(part, 1, 1))


def ring(part, axis):
    return (part, *(shift(part, axis, d) for d in range(1, 4)))


def two_way_gather(mine, other, axis):
    pair = jnp.stack([mine, other])
    high, low = (1, 0) if axis == "row" else (0, 1)
    first, rest = pair[:, :FIRST], pair[:, FIRST:]
    near = jnp.stack(ring(rest, axis))
    first = jnp.stack([first, swap_y(first, high, low)])
    first, near = lax.optimization_barrier((first, near))
    return (*ring(first, axis), near, swap_y(near, high, low))


def z_sum(chunks):
    z = lax.axis_index("col") // 2
    parts = chunks.reshape(4, 4, *chunks.shape[-2:])

    def part_of(d):
        return lax.dynamic_index_in_dim(parts, (z + d) % 4, 0, keepdims=False)

    return ring(add(part_of(0), *(shift(part_of(d), "col", d) for d in range(1, 4))), "col")


def row_exchange(value):
    return lax.all_to_all(value, "row", 0, 0, tiled=True)


def line_exchange(value):
    return lax.all_to_all(value, ("row", "col"), 0, 0, tiled=True, axis_index_groups=LINES)


def on_device(features, weight, bias, cotangent, tile_values, tile_rows, tile_cols, tile_counts):
    tiles = tile_values.reshape(64, 128, 128)
    ids = jnp.concatenate([tile_cols.reshape(64), tile_rows.reshape(64), tile_counts.reshape(1)])
    other_tiles, other_ids = core_swap(tiles), core_swap(ids)
    scale = 1.0 / math.sqrt(65536)
    tables = (ids, other_ids)
    def work(source, loads):
        return dict(
            ids=tables,
            in_specs=[any_spec()] * loads,
            scratch=[
                pltpu.VMEM(source, BF),
                pltpu.VMEM((2, 64, 128, 128), BF),
                pltpu.VMEM((65, 128, HALF), F32),
                pltpu.SemaphoreType.DMA((loads,)),
            ],
            flops=2 * 64 * 128 * 128 * 512,
            moved=16 * 2**20,
        )

    mine, other = call(halves_kernel, (features,), [((512, HALF), BF)] * 2)
    pieces = two_way_gather(mine, core_swap(other), "row")
    (partial,) = call(forward_kernel, (tiles, other_tiles, *pieces), [((64, 128, HALF), BF)], **work((4, 2, 2, 512, HALF), 8))
    parts = line_exchange(partial.reshape(16, 512, HALF))
    output, spread, chunks = call(
        functools.partial(dense_kernel, scale),
        (parts, weight, bias.reshape(1, 512), cotangent),
        [((512, 512), BF), ((16, 512, HALF), BF), ((2, 4, 2, SHARE + TAIL, 512), BF)],
        scratch=[pltpu.VMEM((512, 512), BF), pltpu.VMEM((512, 512), BF), pltpu.VMEM((512, 512), F32)],
        flops=6 * 512**3,
        moved=8 * 2**20,
    )
    spread = line_exchange(spread)
    chunks, spread = lax.optimization_barrier((plane_sum(chunks), spread))
    (back,) = call(backward_kernel, (tiles, other_tiles, spread), [((64, 128, HALF), BF)], **work((16, 512, HALF), 3))
    chunks, back = lax.optimization_barrier((jnp.stack(ring(chunks, "row")), back))
    back = row_exchange(back.reshape(16, 512, HALF))
    chunks = jnp.stack([chunks, core_swap(chunks)])
    weight_grad, bias_grad = call(place_kernel, z_sum(chunks), [((512, 512), F32), ((1, 512), F32)])
    (feature_grad,) = call(final_kernel, (back,), [((512, 512), BF)])
    return (output, feature_grad, weight_grad, bias_grad.reshape(512))


def solution(mesh):
    return jax.shard_map(
        on_device,
        mesh=mesh,
        in_specs=(
            P(("row", "col"), None),
            P(),
            P(),
            P(("row", "col"), None),
            P("row", "col", None, None, None),
            P("row", "col", None),
            P("row", "col", None),
            P("row", "col"),
        ),
        out_specs=(P(("row", "col"), None), P(("row", "col"), None), P(), P()),
        check_vma=False,
    )
```

```python
import functools
import math

import jax
import jax.numpy as jnp
from jax import lax
from jax.experimental import pallas as pl
from jax.experimental.pallas import tpu as pltpu
from jax.sharding import PartitionSpec as P

BF = jnp.bfloat16
F32 = jnp.float32
VMEM_LIMIT = 26 * 2**20
UNROLL = 16
HALF = 256
FIRST = 256
SHARE = 32
TAIL = 16
X_LINES = [[y * 8 + x * 2 + core for x in range(4)] for y in range(2) for core in range(2)]
Z_LINES = [[z * 2 + y for z in range(4)] for y in range(2)]
Y_LINES = [
    [(high * 8 + line) * 8 + z * 2 + low for high in range(2) for low in range(2)] for line in range(8) for z in range(4)
]


def tile_loop(count, acc, step):
    def body(i, carry):
        found = [step(i * UNROLL + j, i * UNROLL + j < count) for j in range(UNROLL)]
        for target, product in found:
            acc[target] += product
        return carry

    lax.fori_loop(0, (count + UNROLL - 1) // UNROLL, body, 0)


def loop(n, step):
    def body(i, carry):
        step(i)
        return carry

    lax.fori_loop(0, n, body, 0)


def start_loads(sources, acc, sems):
    copies = [pltpu.make_async_copy(a, b, sems.at[i]) for i, (a, b) in enumerate(sources)]
    for copy in copies:
        copy.start()

    @functools.partial(loop, acc.shape[0] - 1)
    def _(i):
        acc[i] = jnp.zeros(acc.shape[1:], F32)

    for copy in copies:
        copy.wait()


def halves_kernel(features, mine, other):
    left = lax.axis_index("row") % 2 == 0
    first, second = features[:, :HALF], features[:, HALF:]
    mine[...] = jnp.where(left, first, second)
    other[...] = jnp.where(left, second, first)


def route_loads(pieces, source):
    own, ring_1, ring_2, ring_3, near, far = pieces
    low, high = pl.ds(0, FIRST), pl.ds(FIRST, 512 - FIRST)
    loads = [(piece, source.at[d, :, :, low]) for d, piece in enumerate((own, ring_1, ring_2, ring_3))]
    return loads + [(near, source.at[:, 0, :, high]), (far, source.at[:, 1, :, high])]


def store_parts(acc, outs):
    stay_first, over_y, stay_rest, *ahead = outs
    for d in range(4):
        for y in range(2):
            for core in range(2):
                at = ((d * 2 + y) * 2 + core) * 4
                for b in range(2):
                    rows = slice(b * 128, (b + 1) * 128)
                    (over_y if y else stay_first)[d, core, rows, :] = acc[at + b].astype(BF)
                    (stay_rest if d == 0 else ahead[d - 1])[y, core, rows, :] = acc[at + 2 + b].astype(BF)


def places(k, table, side):
    row_me, col_me = lax.axis_index("row"), lax.axis_index("col")
    col, row = table[k], lax.rem(table[64 + k], 32)
    owner = col // 32
    x = lax.rem(owner // 2, 4) - lax.rem(row_me // 2, 4)
    z = row // 8 - col_me // 2
    col_place = (x, lax.rem(owner // 8 + row_me // 8, 2), lax.rem(owner + row_me, 2), lax.rem(col, 4))
    return col_place, (z, lax.rem(row // 4 + col_me, 2), side, lax.rem(row, 4))


def pick(source, place):
    step, y, core, block = place
    return source[lax.rem(4 - step, 4), y, core, pl.ds(pl.multiple_of(block * 128, 128), 128), :]


def place_in_acc(place, live):
    step, y, core, block = place
    return jnp.where(live, lax.rem(step + 4, 4) * 16 + y * 8 + core * 4 + block, 64)


def tiles_kernel(transposed, ids, other_ids, tiles, other_tiles, *refs):
    pieces, outs, (source, vals, acc, sems) = refs[:6], refs[6:12], refs[12:]
    start_loads([(tiles, vals.at[0]), (other_tiles, vals.at[1]), *route_loads(pieces, source)], acc, sems)
    for side, table in enumerate((ids, other_ids)):

        @functools.partial(tile_loop, table[128], acc)
        def _(k, live, side=side, table=table):
            col_place, row_place = places(k, table, side)
            if transposed:
                product = lax.dot_general(
                    vals[side, k], pick(source, row_place), (((0,), (0,)), ((), ())), preferred_element_type=F32
                )
                return place_in_acc(col_place, live), product
            product = jnp.dot(vals[side, k], pick(source, col_place), preferred_element_type=F32)
            return place_in_acc(row_place, live), product

    store_parts(acc, outs)


def dense_kernel(
    scale, mine, other, weight, bias, cotangent, output, grad_mine, grad_other, chunks, agg, grad_pre, product
):
    size = 128
    core = lax.rem(lax.axis_index("row"), 2)
    left = core == 0

    def body(i, bias_sum):
        at = pl.ds(pl.multiple_of(i * size, size), size)
        a, b = mine[at, :], other[at, :]
        agg[at, :HALF] = jnp.where(left, a, b)
        agg[at, HALF:] = jnp.where(left, b, a)
        pre = jnp.dot(agg[at, :], weight[...], preferred_element_type=F32) + bias[...]
        s = jax.nn.sigmoid(pre)
        output[at, :] = (pre * s).astype(BF)
        grad = (cotangent[at, :].astype(F32) * s * (1.0 + pre * (1.0 - s))).astype(BF)
        grad_pre[at, :] = grad
        back = lax.dot_general(grad, weight[...], (((1,), (1,)), ((), ())), preferred_element_type=F32).astype(BF)
        grad_mine[at, :] = jnp.where(left, back[:, :HALF], back[:, HALF:])
        grad_other[at, :] = jnp.where(left, back[:, HALF:], back[:, :HALF])
        return bias_sum + jnp.sum(grad.astype(F32), axis=0, keepdims=True)

    bias_sum = lax.fori_loop(0, agg.shape[0] // size, body, jnp.zeros((1, agg.shape[1]), F32)) * scale
    product[...] = lax.dot_general(agg[...], grad_pre[...], (((0,), (0,)), ((), ())), preferred_element_type=F32)
    tail = jnp.broadcast_to(bias_sum, (TAIL, agg.shape[1])).astype(BF)
    for far in range(2):
        for x in range(4):
            for y in range(2):
                owner = y * 8 + x * 2 + lax.rem(core + far, 2)
                rows = product[pl.ds(pl.multiple_of(owner * SHARE, SHARE), SHARE), :]
                chunks[far, x, y, :SHARE, :] = (rows * scale).astype(BF)
                chunks[far, x, y, SHARE:, :] = tail


def place_kernel(chunks, weight_grad, bias_grad):
    me = lax.axis_index("row")
    for flat in range(16):
        far, x, y = flat // 8, flat // 2 % 4, flat % 2
        owner = y * 8 + lax.rem(lax.rem(me // 2, 4) + 4 - x, 4) * 2 + lax.rem(me + far, 2)
        at = pl.ds(pl.multiple_of(owner * SHARE, SHARE), SHARE)
        weight_grad[at, :] = chunks[flat // 4, flat % 4, :SHARE, :].astype(F32)
    bias_grad[...] = chunks[0, 0, SHARE : SHARE + 1, :].astype(F32)


def final_kernel(mine, other, out):
    left = lax.axis_index("row") % 2 == 0
    a, b = mine[...], other[...]
    out[:, :HALF] = jnp.where(left, a, b)
    out[:, HALF:] = jnp.where(left, b, a)


def any_spec():
    return pl.BlockSpec(memory_space=pl.ANY)


def vmem_spec():
    return pl.BlockSpec(memory_space=pltpu.VMEM)


def call(kernel, args, out_shape, ids=(), in_specs=None, out_specs=None, scratch=(), flops=0, moved=4 * 2**20):
    shapes = [jax.ShapeDtypeStruct(s, d) for s, d in out_shape]
    return pl.pallas_call(
        kernel,
        grid_spec=pltpu.PrefetchScalarGridSpec(
            num_scalar_prefetch=len(ids),
            in_specs=in_specs or [vmem_spec() for _ in args],
            out_specs=out_specs or [vmem_spec() for _ in shapes],
            scratch_shapes=scratch,
        ),
        out_shape=shapes,
        compiler_params=pltpu.CompilerParams(vmem_limit_bytes=VMEM_LIMIT),
        cost_estimate=pl.CostEstimate(flops=flops, bytes_accessed=moved, transcendentals=0),
    )(*ids, *args)


def core_swap(value):
    return lax.ppermute(value, "row", [(i, i ^ 1) for i in range(16)])


def swap_y(value, high, low):
    to = [(i, i ^ (64 * high + low)) for i in range(128)]
    return lax.ppermute(value, ("row", "col"), to)


def shift(value, axis, d):
    if axis == "row":
        to = [(i, i // 8 * 8 + (i + 2 * d) % 8) for i in range(16)]
    else:
        to = [(i, (i + 2 * d) % 8) for i in range(8)]
    return lax.ppermute(value, axis, to)


def add(*parts):
    total = parts[0].astype(F32)
    for part in parts[1:]:
        total = total + part.astype(F32)
    return total.astype(BF)


def plane_sum(chunks):
    part = add(chunks[0], core_swap(chunks[1]))
    part = add(*lax.all_to_all(part, "row", 0, 0, tiled=True, axis_index_groups=X_LINES))
    return add(*lax.all_to_all(fourfold(part), ("row", "col"), 0, 0, tiled=True, axis_index_groups=Y_LINES))


def fourfold(value):
    return jnp.broadcast_to(value[None], (4, *value.shape))


def ring(part, axis):
    return (part, *(shift(part, axis, d) for d in range(1, 4)))


def two_way_gather(mine, other, axis):
    pair = jnp.stack([mine, other])
    high, low = (1, 0) if axis == "row" else (0, 1)
    first, rest = pair[:, :FIRST], pair[:, FIRST:]
    near = jnp.stack(ring(rest, axis))
    first = jnp.stack([first, swap_y(first, high, low)])
    first, near = lax.optimization_barrier((first, near))
    return (*ring(first, axis), near, swap_y(near, high, low))


def two_way_scatter(parts, axis):
    stay_first, over_y, stay_rest, *ahead = parts
    high, low = (1, 0) if axis == "row" else (0, 1)
    from_y = swap_y(over_y, high, low)
    moved = [shift(part, axis, d + 1) for d, part in enumerate(ahead)]
    rest = [add(stay_rest[y], *(part[y] for part in moved)) for y in range(2)]
    first = [add(stay_first[d], from_y[d]) for d in range(4)]
    first, rest = lax.optimization_barrier((first, rest))
    first = add(first[0], *(shift(first[d], axis, d) for d in range(1, 4)))
    rest = add(rest[0], swap_y(rest[1], high, low))
    total = jnp.concatenate([first, rest], axis=1)
    return total[0], core_swap(total[1])


def z_sum(chunks):
    parts = chunks.reshape(4, 4, *chunks.shape[-2:])
    part = add(*lax.all_to_all(parts, "col", 0, 0, tiled=True, axis_index_groups=Z_LINES))
    return lax.all_to_all(fourfold(part), "col", 0, 0, tiled=True, axis_index_groups=Z_LINES)


def on_device(features, weight, bias, cotangent, tile_values, tile_rows, tile_cols, tile_counts):
    tiles = tile_values.reshape(64, 128, 128)
    ids = jnp.concatenate([tile_cols.reshape(64), tile_rows.reshape(64), tile_counts.reshape(1)])
    other_tiles, other_ids = core_swap(tiles), core_swap(ids)
    scale = 1.0 / math.sqrt(65536)
    tables = (ids, other_ids)
    def multiply(transposed, pieces):
        rest, whole = 512 - FIRST, (4, 2, 2, 512, HALF)
        return call(
            functools.partial(tiles_kernel, transposed),
            (tiles, other_tiles, *pieces),
            [((4, 2, FIRST, HALF), BF)] * 2 + [((2, 2, rest, HALF), BF)] * 4,
            ids=tables,
            in_specs=[any_spec()] * 8,
            scratch=[
                pltpu.VMEM(whole, BF),
                pltpu.VMEM((2, 64, 128, 128), BF),
                pltpu.VMEM((65, 128, HALF), F32),
                pltpu.SemaphoreType.DMA((8,)),
            ],
            flops=2 * 64 * 128 * 128 * 512,
            moved=16 * 2**20,
        )

    mine, other = call(halves_kernel, (features,), [((512, HALF), BF)] * 2)
    pieces = two_way_gather(mine, core_swap(other), "row")
    mine, other = two_way_scatter(multiply(False, pieces), "col")
    output, mine, other, chunks = call(
        functools.partial(dense_kernel, scale),
        (mine, other, weight, bias.reshape(1, 512), cotangent),
        [((512, 512), BF), ((512, HALF), BF), ((512, HALF), BF), ((2, 4, 2, SHARE + TAIL, 512), BF)],
        scratch=[pltpu.VMEM((512, 512), BF), pltpu.VMEM((512, 512), BF), pltpu.VMEM((512, 512), F32)],
        flops=6 * 512**3,
        moved=8 * 2**20,
    )
    pieces = two_way_gather(mine, core_swap(other), "col")
    chunks, pieces = lax.optimization_barrier((plane_sum(chunks), pieces))
    parts = multiply(True, pieces)
    chunks, parts = lax.optimization_barrier((jnp.stack(ring(chunks, "row")), parts))
    mine, other = two_way_scatter(parts, "row")
    chunks = jnp.stack([chunks, core_swap(chunks)])
    weight_grad, bias_grad = call(place_kernel, (z_sum(chunks),), [((512, 512), F32), ((1, 512), F32)])
    (feature_grad,) = call(final_kernel, (mine, other), [((512, 512), BF)])
    return (output, feature_grad, weight_grad, bias_grad.reshape(512))


def solution(mesh):
    return jax.shard_map(
        on_device,
        mesh=mesh,
        in_specs=(
            P(("row", "col"), None),
            P(),
            P(),
            P(("row", "col"), None),
            P("row", "col", None, None, None),
            P("row", "col", None),
            P("row", "col", None),
            P("row", "col"),
        ),
        out_specs=(P(("row", "col"), None), P(("row", "col"), None), P(), P()),
        check_vma=False,
    )
```

```python
import functools
import math

import jax
import jax.numpy as jnp
from jax import lax
from jax.experimental import pallas as pl
from jax.experimental.pallas import tpu as pltpu
from jax.sharding import PartitionSpec as P

BF = jnp.bfloat16
F32 = jnp.float32
UNROLL = 16
TILES_VMEM = 18 * 2**20
HALF = 256
FIRST = 256
SHARE = 32
TAIL = 16
X_LINES = [[y * 8 + x * 2 + core for x in range(4)] for y in range(2) for core in range(2)]
Z_LINES = [[z * 2 + y for z in range(4)] for y in range(2)]
Y_LINES = [
    [(high * 8 + line) * 8 + z * 2 + low for high in range(2) for low in range(2)] for line in range(8) for z in range(4)
]


def tile_loop(count, acc, step):
    def body(i, carry):
        found = [step(i * UNROLL + j, i * UNROLL + j < count) for j in range(UNROLL)]
        for target, product in found:
            acc[target] += product
        return carry

    lax.fori_loop(0, (count + UNROLL - 1) // UNROLL, body, 0)


def loop(n, step):
    def body(i, carry):
        step(i)
        return carry

    lax.fori_loop(0, n, body, 0)


def start_loads(sources, acc, sems):
    copies = [pltpu.make_async_copy(a, b, sems.at[i]) for i, (a, b) in enumerate(sources)]
    for copy in copies:
        copy.start()

    @functools.partial(loop, acc.shape[0] - 1)
    def _(i):
        acc[i] = jnp.zeros(acc.shape[1:], F32)

    for copy in copies:
        copy.wait()


def halves_kernel(features, mine, other):
    left = lax.axis_index("row") % 2 == 0
    first, second = features[:, :HALF], features[:, HALF:]
    mine[...] = jnp.where(left, first, second)
    other[...] = jnp.where(left, second, first)


def store_parts(acc, outs):
    stay_first, over_y, stay_rest, *ahead = outs
    for d in range(4):
        for y in range(2):
            for core in range(2):
                at = ((d * 2 + y) * 2 + core) * 4
                for b in range(2):
                    rows = slice(b * 128, (b + 1) * 128)
                    (over_y if y else stay_first)[d, core, rows, :] = acc[at + b].astype(BF)
                    (stay_rest if d == 0 else ahead[d - 1])[y, core, rows, :] = acc[at + 2 + b].astype(BF)


def places(k, table, side):
    row_me, col_me = lax.axis_index("row"), lax.axis_index("col")
    col, row = table[k], lax.rem(table[64 + k], 32)
    owner = col // 32
    x = lax.rem(owner // 2, 4) - lax.rem(row_me // 2, 4)
    z = row // 8 - col_me // 2
    col_place = (x, lax.rem(owner // 8 + row_me // 8, 2), lax.rem(owner + row_me, 2), lax.rem(col, 4))
    return col_place, (z, lax.rem(row // 4 + col_me, 2), side, lax.rem(row, 4))


def pick(source, place):
    step, y, core, block = place
    return source[lax.rem(4 - step, 4), y, core, pl.ds(pl.multiple_of(block * 128, 128), 128), :]


def place_in_acc(place, live):
    step, y, core, block = place
    return jnp.where(live, lax.rem(step + 4, 4) * 16 + y * 8 + core * 4 + block, 64)


def tiles_kernel(transposed, ids, other_ids, tiles, other_tiles, *refs):
    source, outs, (vals, acc, sems) = refs[0], refs[1:7], refs[7:]
    start_loads([(tiles, vals.at[0]), (other_tiles, vals.at[1])], acc, sems)
    for side, table in enumerate((ids, other_ids)):

        @functools.partial(tile_loop, table[128], acc)
        def _(k, live, side=side, table=table):
            col_place, row_place = places(k, table, side)
            if transposed:
                product = lax.dot_general(
                    vals[side, k], pick(source, row_place), (((0,), (0,)), ((), ())), preferred_element_type=F32
                )
                return place_in_acc(col_place, live), product
            product = jnp.dot(vals[side, k], pick(source, col_place), preferred_element_type=F32)
            return place_in_acc(row_place, live), product

    store_parts(acc, outs)


def dense_kernel(start, mine, other, weight, bias, cotangent, output, grad_mine, grad_other, agg, grad_pre):
    left = lax.rem(lax.axis_index("row"), 2) == 0
    size = 128
    for i in range(mine.shape[0] // size):
        at = slice(i * size, (i + 1) * size)
        a, b = mine[at, :], other[at, :]
        agg[at, :HALF] = jnp.where(left, a, b)
        agg[at, HALF:] = jnp.where(left, b, a)
        pre = jnp.dot(agg[at, :], weight[...], preferred_element_type=F32) + bias[...]
        s = jax.nn.sigmoid(pre)
        output[at, :] = (pre * s).astype(BF)
        given = cotangent[start + i * size : start + (i + 1) * size, :].astype(F32)
        grad = (given * s * (1.0 + pre * (1.0 - s))).astype(BF)
        grad_pre[at, :] = grad
        back = lax.dot_general(grad, weight[...], (((1,), (1,)), ((), ())), preferred_element_type=F32).astype(BF)
        grad_mine[at, :] = jnp.where(left, back[:, :HALF], back[:, HALF:])
        grad_other[at, :] = jnp.where(left, back[:, HALF:], back[:, :HALF])


def weight_kernel(scale, agg_1, agg_2, grad_1, grad_2, chunks, product):
    core = lax.rem(lax.axis_index("row"), 2)
    both = (((0,), (0,)), ((), ()))
    product[...] = lax.dot_general(agg_1[...], grad_1[...], both, preferred_element_type=F32)
    product[...] += lax.dot_general(agg_2[...], grad_2[...], both, preferred_element_type=F32)
    bias_sum = jnp.sum(grad_1[...].astype(F32), axis=0, keepdims=True)
    bias_sum = (bias_sum + jnp.sum(grad_2[...].astype(F32), axis=0, keepdims=True)) * scale
    tail = jnp.broadcast_to(bias_sum, (TAIL, bias_sum.shape[1])).astype(BF)
    for far in range(2):
        for x in range(4):
            for y in range(2):
                owner = y * 8 + x * 2 + lax.rem(core + far, 2)
                rows = product[pl.ds(pl.multiple_of(owner * SHARE, SHARE), SHARE), :]
                chunks[far, x, y, :SHARE, :] = (rows * scale).astype(BF)
                chunks[far, x, y, SHARE:, :] = tail


def place_kernel(chunks, weight_grad, bias_grad):
    me = lax.axis_index("row")
    for flat in range(16):
        far, x, y = flat // 8, flat // 2 % 4, flat % 2
        owner = y * 8 + lax.rem(lax.rem(me // 2, 4) + 4 - x, 4) * 2 + lax.rem(me + far, 2)
        at = pl.ds(pl.multiple_of(owner * SHARE, SHARE), SHARE)
        weight_grad[at, :] = chunks[flat // 4, flat % 4, :SHARE, :].astype(F32)
    bias_grad[...] = chunks[0, 0, SHARE : SHARE + 1, :].astype(F32)


def final_kernel(first_mine, first_other, rest_mine, rest_other, out):
    left = lax.axis_index("row") % 2 == 0
    for rows, mine, other in ((slice(0, FIRST), first_mine, first_other), (slice(FIRST, 512), rest_mine, rest_other)):
        a, b = mine[...], other[...]
        out[rows, :HALF] = jnp.where(left, a, b)
        out[rows, HALF:] = jnp.where(left, b, a)


def any_spec():
    return pl.BlockSpec(memory_space=pl.ANY)


def vmem_spec():
    return pl.BlockSpec(memory_space=pltpu.VMEM)


def call(kernel, args, out_shape, ids=(), in_specs=None, scratch=(), flops=0, moved=4 * 2**20, vmem=8 * 2**20):
    shapes = [jax.ShapeDtypeStruct(s, d) for s, d in out_shape]
    return pl.pallas_call(
        kernel,
        grid_spec=pltpu.PrefetchScalarGridSpec(
            num_scalar_prefetch=len(ids),
            in_specs=in_specs or [vmem_spec() for _ in args],
            out_specs=[vmem_spec() for _ in shapes],
            scratch_shapes=scratch,
        ),
        out_shape=shapes,
        compiler_params=pltpu.CompilerParams(vmem_limit_bytes=vmem),
        cost_estimate=pl.CostEstimate(flops=flops, bytes_accessed=moved, transcendentals=0),
    )(*ids, *args)


def core_swap(value):
    return lax.ppermute(value, "row", [(i, i ^ 1) for i in range(16)])


def swap_y(value, high, low):
    to = [(i, i ^ (64 * high + low)) for i in range(128)]
    return lax.ppermute(value, ("row", "col"), to)


def shift(value, axis, d):
    if axis == "row":
        to = [(i, i // 8 * 8 + (i + 2 * d) % 8) for i in range(16)]
    else:
        to = [(i, (i + 2 * d) % 8) for i in range(8)]
    return lax.ppermute(value, axis, to)


def add(*parts):
    total = parts[0].astype(F32)
    for part in parts[1:]:
        total = total + part.astype(F32)
    return total.astype(BF)


def plane_sum(chunks):
    part = add(chunks[0], core_swap(chunks[1]))
    part = add(*lax.all_to_all(part, "row", 0, 0, tiled=True, axis_index_groups=X_LINES))
    return add(*lax.all_to_all(fourfold(part), ("row", "col"), 0, 0, tiled=True, axis_index_groups=Y_LINES))


def fourfold(value):
    return jnp.broadcast_to(value[None], (4, *value.shape))


def ring(part, axis):
    return (part, *(shift(part, axis, d) for d in range(1, 4)))


def two_way_gather(first, rest, axis):
    high, low = (1, 0) if axis == "row" else (0, 1)
    near = jnp.stack(ring(rest, axis))
    first = jnp.stack([first, swap_y(first, high, low)])
    first, near = lax.optimization_barrier((first, near))
    far = swap_y(near, high, low)
    return jnp.concatenate([jnp.stack(ring(first, axis)), jnp.stack([near, far], axis=1)], axis=3)


def two_way_scatter(parts, axis):
    stay_first, over_y, stay_rest, *ahead = parts
    high, low = (1, 0) if axis == "row" else (0, 1)
    from_y = swap_y(over_y, high, low)
    moved = [shift(part, axis, d + 1) for d, part in enumerate(ahead)]
    rest = [add(stay_rest[y], *(part[y] for part in moved)) for y in range(2)]
    first = [add(stay_first[d], from_y[d]) for d in range(4)]
    first, rest = lax.optimization_barrier((first, rest))
    first = add(first[0], *(shift(first[d], axis, d) for d in range(1, 4)))
    rest = add(rest[0], swap_y(rest[1], high, low))
    return (first[0], core_swap(first[1])), (rest[0], core_swap(rest[1]))


def z_sum(chunks):
    parts = chunks.reshape(4, 4, *chunks.shape[-2:])
    part = add(*lax.all_to_all(parts, "col", 0, 0, tiled=True, axis_index_groups=Z_LINES))
    return lax.all_to_all(fourfold(part), "col", 0, 0, tiled=True, axis_index_groups=Z_LINES)


def on_device(features, weight, bias, cotangent, tile_values, tile_rows, tile_cols, tile_counts):
    tiles = tile_values.reshape(64, 128, 128)
    ids = jnp.concatenate([tile_cols.reshape(64), tile_rows.reshape(64), tile_counts.reshape(1)])
    other_tiles, other_ids = core_swap(tiles), core_swap(ids)
    scale = 1.0 / math.sqrt(65536)
    tables = (ids, other_ids)
    def multiply(transposed, source):
        rest = 512 - FIRST
        return call(
            functools.partial(tiles_kernel, transposed),
            (tiles, other_tiles, source),
            [((4, 2, FIRST, HALF), BF)] * 2 + [((2, 2, rest, HALF), BF)] * 4,
            ids=tables,
            in_specs=[any_spec(), any_spec(), vmem_spec()],
            scratch=[
                pltpu.VMEM((2, 64, 128, 128), BF),
                pltpu.VMEM((65, 128, HALF), F32),
                pltpu.SemaphoreType.DMA((2,)),
            ],
            flops=2 * 64 * 128 * 128 * 512,
            moved=16 * 2**20,
            vmem=TILES_VMEM,
        )

    def dense(start, halves):
        rows = halves[0].shape[0]
        return call(
            functools.partial(dense_kernel, start),
            (*halves, weight, bias.reshape(1, 512), cotangent),
            [((rows, 512), BF), ((rows, HALF), BF), ((rows, HALF), BF), ((rows, 512), BF), ((rows, 512), BF)],
            flops=4 * rows * 512**2,
        )

    mine, other = call(halves_kernel, (features,), [((512, HALF), BF)] * 2)
    pair = jnp.stack([mine, core_swap(other)])
    source = two_way_gather(pair[:, :FIRST], pair[:, FIRST:], "row")
    first, rest = two_way_scatter(multiply(False, source), "col")
    rest_output, mine, other, rest_agg, rest_grad = dense(FIRST, rest)
    rest = jnp.stack([mine, core_swap(other)])
    first_output, mine, other, first_agg, first_grad = dense(0, first)
    first = jnp.stack([mine, core_swap(other)])
    output = jnp.concatenate([first_output, rest_output])
    source = two_way_gather(first, rest, "col")
    (chunks,) = call(
        functools.partial(weight_kernel, scale),
        (first_agg, rest_agg, first_grad, rest_grad),
        [((2, 4, 2, SHARE + TAIL, 512), BF)],
        scratch=[pltpu.VMEM((512, 512), F32)],
        flops=2 * 512**3,
    )
    chunks, source = lax.optimization_barrier((plane_sum(chunks), source))
    parts = multiply(True, source)
    chunks, parts = lax.optimization_barrier((jnp.stack(ring(chunks, "row")), parts))
    first, rest = two_way_scatter(parts, "row")
    chunks = jnp.stack([chunks, core_swap(chunks)])
    weight_grad, bias_grad = call(place_kernel, (z_sum(chunks),), [((512, 512), F32), ((1, 512), F32)])
    (feature_grad,) = call(final_kernel, (*first, *rest), [((512, 512), BF)])
    return (output, feature_grad, weight_grad, bias_grad.reshape(512))


def solution(mesh):
    return jax.shard_map(
        on_device,
        mesh=mesh,
        in_specs=(
            P(("row", "col"), None),
            P(),
            P(),
            P(("row", "col"), None),
            P("row", "col", None, None, None),
            P("row", "col", None),
            P("row", "col", None),
            P("row", "col"),
        ),
        out_specs=(P(("row", "col"), None), P(("row", "col"), None), P(), P()),
        check_vma=False,
    )
```

```python
import functools
import math

import jax
import jax.numpy as jnp
from jax import lax
from jax.experimental import pallas as pl
from jax.experimental.pallas import tpu as pltpu
from jax.sharding import PartitionSpec as P

BF = jnp.bfloat16
F32 = jnp.float32
UNROLL = 16
TILES_VMEM = 18 * 2**20
HALF = 256
FIRST = 256
SHARE = 32
TAIL = 16
CHUNK = 2 * SHARE + TAIL


def tile_loop(count, acc, step):
    def body(i, carry):
        found = [step(i * UNROLL + j, i * UNROLL + j < count) for j in range(UNROLL)]
        for target, product in found:
            acc[target] += product
        return carry

    lax.fori_loop(0, (count + UNROLL - 1) // UNROLL, body, 0)


def loop(n, step):
    def body(i, carry):
        step(i)
        return carry

    lax.fori_loop(0, n, body, 0)


def start_loads(sources, acc, sems):
    copies = [pltpu.make_async_copy(a, b, sems.at[i]) for i, (a, b) in enumerate(sources)]
    for copy in copies:
        copy.start()

    @functools.partial(loop, acc.shape[0] - 1)
    def _(i):
        acc[i] = jnp.zeros(acc.shape[1:], F32)

    for copy in copies:
        copy.wait()


def halves_kernel(features, mine, other):
    left = lax.axis_index("row") % 2 == 0
    first, second = features[:, :HALF], features[:, HALF:]
    mine[...] = jnp.where(left, first, second)
    other[...] = jnp.where(left, second, first)


def store_parts(acc, outs):
    stay_first, over_y, stay_rest, *ahead = outs
    for d in range(4):
        for y in range(2):
            for core in range(2):
                at = ((d * 2 + y) * 2 + core) * 4
                for b in range(2):
                    rows = slice(b * 128, (b + 1) * 128)
                    (over_y if y else stay_first)[d, core, rows, :] = acc[at + b].astype(BF)
                    (stay_rest if d == 0 else ahead[d - 1])[y, core, rows, :] = acc[at + 2 + b].astype(BF)


def places(k, table, side):
    row_me, col_me = lax.axis_index("row"), lax.axis_index("col")
    col, row = table[k], lax.rem(table[64 + k], 32)
    owner = col // 32
    x = lax.rem(owner // 2, 4) - lax.rem(row_me // 2, 4)
    z = row // 8 - col_me // 2
    col_place = (x, lax.rem(owner // 8 + row_me // 8, 2), lax.rem(owner + row_me, 2), lax.rem(col, 4))
    return col_place, (z, lax.rem(row // 4 + col_me, 2), side, lax.rem(row, 4))


def pick(source, place):
    step, y, core, block = place
    return source[lax.rem(4 - step, 4), y, core, pl.ds(pl.multiple_of(block * 128, 128), 128), :]


def place_in_acc(place, live):
    step, y, core, block = place
    return jnp.where(live, lax.rem(step + 4, 4) * 16 + y * 8 + core * 4 + block, 64)


def tiles_kernel(transposed, ids, other_ids, tiles, other_tiles, *refs):
    source, outs, (vals, acc, sems) = refs[0], refs[1:7], refs[7:]
    start_loads([(tiles, vals.at[0]), (other_tiles, vals.at[1])], acc, sems)
    for side, table in enumerate((ids, other_ids)):

        @functools.partial(tile_loop, table[128], acc)
        def _(k, live, side=side, table=table):
            col_place, row_place = places(k, table, side)
            if transposed:
                product = lax.dot_general(
                    vals[side, k], pick(source, row_place), (((0,), (0,)), ((), ())), preferred_element_type=F32
                )
                return place_in_acc(col_place, live), product
            product = jnp.dot(vals[side, k], pick(source, col_place), preferred_element_type=F32)
            return place_in_acc(row_place, live), product

    store_parts(acc, outs)


def dense_kernel(start, mine, other, weight, bias, cotangent, output, grad_mine, grad_other, agg, grad_pre):
    left = lax.rem(lax.axis_index("row"), 2) == 0
    size = 128
    for i in range(mine.shape[0] // size):
        at = slice(i * size, (i + 1) * size)
        a, b = mine[at, :], other[at, :]
        agg[at, :HALF] = jnp.where(left, a, b)
        agg[at, HALF:] = jnp.where(left, b, a)
        pre = jnp.dot(agg[at, :], weight[...], preferred_element_type=F32) + bias[...]
        s = jax.nn.sigmoid(pre)
        output[at, :] = (pre * s).astype(BF)
        given = cotangent[start + i * size : start + (i + 1) * size, :].astype(F32)
        grad = (given * s * (1.0 + pre * (1.0 - s))).astype(BF)
        grad_pre[at, :] = grad
        back = lax.dot_general(grad, weight[...], (((1,), (1,)), ((), ())), preferred_element_type=F32).astype(BF)
        grad_mine[at, :] = jnp.where(left, back[:, :HALF], back[:, HALF:])
        grad_other[at, :] = jnp.where(left, back[:, HALF:], back[:, :HALF])


def weight_kernel(scale, agg_1, agg_2, grad_1, grad_2, chunks, product):
    core = lax.rem(lax.axis_index("row"), 2)
    col = lax.axis_index("col")
    both = (((0,), (0,)), ((), ()))
    product[...] = lax.dot_general(agg_1[...], grad_1[...], both, preferred_element_type=F32)
    product[...] += lax.dot_general(agg_2[...], grad_2[...], both, preferred_element_type=F32)
    bias_sum = jnp.sum(grad_1[...].astype(F32), axis=0, keepdims=True)
    bias_sum = (bias_sum + jnp.sum(grad_2[...].astype(F32), axis=0, keepdims=True)) * scale
    row = lax.broadcasted_iota(jnp.int32, (TAIL, HALF), 0)
    tail = jnp.where(row == 0, bias_sum[:, :HALF], jnp.where(row == 1, bias_sum[:, HALF:], 0.0)).astype(BF)
    for far in range(2):
        for d in range(4):
            for y in range(2):
                rows = product[share_rows(lax.rem(core + far, 2), lax.rem(col // 2 + d, 4), lax.rem(col + y, 2)), :]
                rows = (rows * scale).astype(BF)
                chunks[far, d, y, :SHARE, :] = rows[:, :HALF]
                chunks[far, d, y, SHARE : 2 * SHARE, :] = rows[:, HALF:]
                chunks[far, d, y, 2 * SHARE :, :] = tail


def share_rows(core, z, y):
    return pl.ds(pl.multiple_of((core * 8 + z * 2 + y) * SHARE, SHARE), SHARE)


def place_kernel(own, moved_1, moved_2, moved_3, weight_grad, bias_grad):
    core = lax.rem(lax.axis_index("row"), 2)
    col = lax.axis_index("col")
    for d, piece in enumerate((own, moved_1, moved_2, moved_3)):
        for y in range(2):
            for far in range(2):
                at = share_rows(lax.rem(core + far, 2), lax.rem(col // 2 + 4 - d, 4), lax.rem(col + y, 2))
                weight_grad[at, :HALF] = piece[y, far, :SHARE, :].astype(F32)
                weight_grad[at, HALF:] = piece[y, far, SHARE : 2 * SHARE, :].astype(F32)
    bias_grad[:, :HALF] = own[0, 0, 2 * SHARE : 2 * SHARE + 1, :].astype(F32)
    bias_grad[:, HALF:] = own[0, 0, 2 * SHARE + 1 : 2 * SHARE + 2, :].astype(F32)


def final_kernel(first_mine, first_other, rest_mine, rest_other, out):
    left = lax.axis_index("row") % 2 == 0
    for rows, mine, other in ((slice(0, FIRST), first_mine, first_other), (slice(FIRST, 512), rest_mine, rest_other)):
        a, b = mine[...], other[...]
        out[rows, :HALF] = jnp.where(left, a, b)
        out[rows, HALF:] = jnp.where(left, b, a)


def any_spec():
    return pl.BlockSpec(memory_space=pl.ANY)


def vmem_spec():
    return pl.BlockSpec(memory_space=pltpu.VMEM)


def call(kernel, args, out_shape, ids=(), in_specs=None, scratch=(), flops=0, moved=4 * 2**20, vmem=8 * 2**20):
    shapes = [jax.ShapeDtypeStruct(s, d) for s, d in out_shape]
    return pl.pallas_call(
        kernel,
        grid_spec=pltpu.PrefetchScalarGridSpec(
            num_scalar_prefetch=len(ids),
            in_specs=in_specs or [vmem_spec() for _ in args],
            out_specs=[vmem_spec() for _ in shapes],
            scratch_shapes=scratch,
        ),
        out_shape=shapes,
        compiler_params=pltpu.CompilerParams(vmem_limit_bytes=vmem),
        cost_estimate=pl.CostEstimate(flops=flops, bytes_accessed=moved, transcendentals=0),
    )(*ids, *args)


def core_swap(value):
    return lax.ppermute(value, "row", [(i, i ^ 1) for i in range(16)])


def swap_y(value, high, low):
    to = [(i, i ^ (64 * high + low)) for i in range(128)]
    return lax.ppermute(value, ("row", "col"), to)


def shift(value, axis, d):
    if axis == "row":
        to = [(i, i // 8 * 8 + (i + 2 * d) % 8) for i in range(16)]
    else:
        to = [(i, (i + 2 * d) % 8) for i in range(8)]
    return lax.ppermute(value, axis, to)


def add(*parts):
    total = parts[0].astype(F32)
    for part in parts[1:]:
        total = total + part.astype(F32)
    return total.astype(BF)


def ring(part, axis):
    return (part, *(shift(part, axis, d) for d in range(1, 4)))


def two_way_gather(first, rest, axis, chunks=None):
    high, low = (1, 0) if axis == "row" else (0, 1)
    near = jnp.stack(ring(rest, axis))
    if chunks is None:
        other = swap_y(first, high, low)
    else:
        moved = swap_y(jnp.concatenate([first, chunks[:, 1].reshape(2, 2 * CHUNK, HALF)], axis=1), high, low)
        other = moved[:, :FIRST]
        chunks = add(chunks[:, 0], moved[:, FIRST:].reshape(4, CHUNK, HALF))
    first = jnp.stack([first, other])
    first, near, chunks = lax.optimization_barrier((first, near, chunks))
    far = swap_y(near, high, low)
    if chunks is None:
        pieces = ring(first, axis)
    else:
        flat = first.reshape(-1, HALF)
        size = flat.shape[0]
        moved = [shift(jnp.concatenate([flat, chunks[d]]), axis, d) for d in range(1, 4)]
        pieces = (first, *(part[:size].reshape(first.shape) for part in moved))
        chunks = add(chunks[0], *(part[size:] for part in moved))
    return jnp.concatenate([jnp.stack(pieces), jnp.stack([near, far], axis=1)], axis=3), chunks


def two_way_scatter(parts, axis, chunk=None):
    stay_first, over_y, stay_rest, *ahead = parts
    high, low = (1, 0) if axis == "row" else (0, 1)
    if chunk is None:
        from_y = swap_y(over_y, high, low)
    else:
        flat = over_y.reshape(-1, HALF)
        size = flat.shape[0]
        moved = swap_y(jnp.concatenate([flat, chunk]), high, low)
        from_y = moved[:size].reshape(over_y.shape)
        chunk = add(chunk, moved[size:])
    moved = [shift(part, axis, d + 1) for d, part in enumerate(ahead)]
    rest = [add(stay_rest[y], *(part[y] for part in moved)) for y in range(2)]
    first = [add(stay_first[d], from_y[d]) for d in range(4)]
    first, rest = lax.optimization_barrier((first, rest))
    first = add(first[0], *(shift(first[d], axis, d) for d in range(1, 4)))
    rest = add(rest[0], swap_y(rest[1], high, low))
    return (first[0], core_swap(first[1])), (rest[0], core_swap(rest[1])), chunk


def on_device(features, weight, bias, cotangent, tile_values, tile_rows, tile_cols, tile_counts):
    tiles = tile_values.reshape(64, 128, 128)
    ids = jnp.concatenate([tile_cols.reshape(64), tile_rows.reshape(64), tile_counts.reshape(1)])
    other_tiles, other_ids = core_swap(tiles), core_swap(ids)
    scale = 1.0 / math.sqrt(65536)
    tables = (ids, other_ids)
    def multiply(transposed, source):
        rest = 512 - FIRST
        return call(
            functools.partial(tiles_kernel, transposed),
            (tiles, other_tiles, source),
            [((4, 2, FIRST, HALF), BF)] * 2 + [((2, 2, rest, HALF), BF)] * 4,
            ids=tables,
            in_specs=[any_spec(), any_spec(), vmem_spec()],
            scratch=[
                pltpu.VMEM((2, 64, 128, 128), BF),
                pltpu.VMEM((65, 128, HALF), F32),
                pltpu.SemaphoreType.DMA((2,)),
            ],
            flops=2 * 64 * 128 * 128 * 512,
            moved=16 * 2**20,
            vmem=TILES_VMEM,
        )

    def dense(start, halves):
        rows = halves[0].shape[0]
        return call(
            functools.partial(dense_kernel, start),
            (*halves, weight, bias.reshape(1, 512), cotangent),
            [((rows, 512), BF), ((rows, HALF), BF), ((rows, HALF), BF), ((rows, 512), BF), ((rows, 512), BF)],
            flops=4 * rows * 512**2,
        )

    mine, other = call(halves_kernel, (features,), [((512, HALF), BF)] * 2)
    pair = jnp.stack([mine, core_swap(other)])
    source, _ = two_way_gather(pair[:, :FIRST], pair[:, FIRST:], "row")
    first, rest, _ = two_way_scatter(multiply(False, source), "col")
    rest_output, mine, other, rest_agg, rest_grad = dense(FIRST, rest)
    rest = jnp.stack([mine, core_swap(other)])
    first_output, mine, other, first_agg, first_grad = dense(0, first)
    first = jnp.stack([mine, core_swap(other)])
    output = jnp.concatenate([first_output, rest_output])
    (chunks,) = call(
        functools.partial(weight_kernel, scale),
        (first_agg, rest_agg, first_grad, rest_grad),
        [((2, 4, 2, CHUNK, HALF), BF)],
        scratch=[pltpu.VMEM((512, 512), F32)],
        flops=2 * 512**3,
    )
    chunks = add(chunks[0], core_swap(chunks[1]))
    source, chunk = two_way_gather(first, rest, "col", chunks)
    source, chunk = lax.optimization_barrier((source, chunk))
    parts = multiply(True, source)
    chunk, parts = lax.optimization_barrier((add(*ring(chunk, "row")), parts))
    first, rest, chunk = two_way_scatter(parts, "row", chunk)
    chunks = jnp.stack([chunk, core_swap(chunk)])
    chunks = jnp.stack([chunks, swap_y(chunks, 0, 1)])
    weight_grad, bias_grad = call(place_kernel, ring(chunks, "col"), [((512, 512), F32), ((1, 512), F32)])
    (feature_grad,) = call(final_kernel, (*first, *rest), [((512, 512), BF)])
    return (output, feature_grad, weight_grad, bias_grad.reshape(512))


def solution(mesh):
    return jax.shard_map(
        on_device,
        mesh=mesh,
        in_specs=(
            P(("row", "col"), None),
            P(),
            P(),
            P(("row", "col"), None),
            P("row", "col", None, None, None),
            P("row", "col", None),
            P("row", "col", None),
            P("row", "col"),
        ),
        out_specs=(P(("row", "col"), None), P(("row", "col"), None), P(), P()),
        check_vma=False,
    )
```

```python
import functools
import math

import jax
import jax.numpy as jnp
from jax import lax
from jax.experimental import pallas as pl
from jax.experimental.pallas import tpu as pltpu
from jax.sharding import PartitionSpec as P

BF = jnp.bfloat16
F32 = jnp.float32
UNROLL = 16
TILES_VMEM = 18 * 2**20
HALF = 256
FIRST = 256
SHARE = 32
TAIL = 16
CHUNK = 2 * SHARE + TAIL


def tile_loop(count, acc, step):
    def body(i, carry):
        found = [step(i * UNROLL + j, i * UNROLL + j < count) for j in range(UNROLL)]
        for target, product in found:
            acc[target] += product
        return carry

    lax.fori_loop(0, (count + UNROLL - 1) // UNROLL, body, 0)


def loop(n, step):
    def body(i, carry):
        step(i)
        return carry

    lax.fori_loop(0, n, body, 0)


def start_loads(sources, acc, sems):
    copies = [pltpu.make_async_copy(a, b, sems.at[i]) for i, (a, b) in enumerate(sources)]
    for copy in copies:
        copy.start()

    @functools.partial(loop, acc.shape[0] - 1)
    def _(i):
        acc[i] = jnp.zeros(acc.shape[1:], F32)

    for copy in copies:
        copy.wait()


def halves_kernel(features, mine, other):
    left = lax.axis_index("row") % 2 == 0
    first, second = features[:, :HALF], features[:, HALF:]
    mine[...] = jnp.where(left, first, second)
    other[...] = jnp.where(left, second, first)


def store_parts(acc, outs):
    stay_first, over_y, stay_rest, *ahead = outs
    for d in range(4):
        for y in range(2):
            for core in range(2):
                at = ((d * 2 + y) * 2 + core) * 4
                for b in range(2):
                    rows = slice(b * 128, (b + 1) * 128)
                    (over_y if y else stay_first)[d, core, rows, :] = acc[at + b].astype(BF)
                    (stay_rest if d == 0 else ahead[d - 1])[y, core, rows, :] = acc[at + 2 + b].astype(BF)


def places(k, table, side):
    row_me, col_me = lax.axis_index("row"), lax.axis_index("col")
    col, row = table[k], lax.rem(table[64 + k], 32)
    owner = col // 32
    x = lax.rem(owner // 2, 4) - lax.rem(row_me // 2, 4)
    z = row // 8 - col_me // 2
    col_place = (x, lax.rem(owner // 8 + row_me // 8, 2), lax.rem(owner + row_me, 2), lax.rem(col, 4))
    return col_place, (z, lax.rem(row // 4 + col_me, 2), side, lax.rem(row, 4))


def pick(source, place):
    step, y, core, block = place
    return source[lax.rem(4 - step, 4), y, core, pl.ds(pl.multiple_of(block * 128, 128), 128), :]


def place_in_acc(place, live):
    step, y, core, block = place
    return jnp.where(live, lax.rem(step + 4, 4) * 16 + y * 8 + core * 4 + block, 64)


def tiles_kernel(transposed, ids, other_ids, tiles, other_tiles, *refs):
    source, outs, (vals, acc, sems) = refs[0], refs[1:7], refs[7:]
    start_loads([(tiles, vals.at[0]), (other_tiles, vals.at[1])], acc, sems)
    for side, table in enumerate((ids, other_ids)):

        @functools.partial(tile_loop, table[128], acc)
        def _(k, live, side=side, table=table):
            col_place, row_place = places(k, table, side)
            if transposed:
                product = lax.dot_general(
                    vals[side, k], pick(source, row_place), (((0,), (0,)), ((), ())), preferred_element_type=F32
                )
                return place_in_acc(col_place, live), product
            product = jnp.dot(vals[side, k], pick(source, col_place), preferred_element_type=F32)
            return place_in_acc(row_place, live), product

    store_parts(acc, outs)


def dense_kernel(start, mine, other, weight, bias, cotangent, output, grad_mine, grad_other, agg, grad_pre):
    left = lax.rem(lax.axis_index("row"), 2) == 0
    size = 128
    for i in range(mine.shape[0] // size):
        at = slice(i * size, (i + 1) * size)
        a, b = mine[at, :], other[at, :]
        agg[at, :HALF] = jnp.where(left, a, b)
        agg[at, HALF:] = jnp.where(left, b, a)
        pre = jnp.dot(agg[at, :], weight[...], preferred_element_type=F32) + bias[...]
        s = jax.nn.sigmoid(pre)
        output[at, :] = (pre * s).astype(BF)
        given = cotangent[start + i * size : start + (i + 1) * size, :].astype(F32)
        grad = (given * s * (1.0 + pre * (1.0 - s))).astype(BF)
        grad_pre[at, :] = grad
        back = lax.dot_general(grad, weight[...], (((1,), (1,)), ((), ())), preferred_element_type=F32).astype(BF)
        grad_mine[at, :] = jnp.where(left, back[:, :HALF], back[:, HALF:])
        grad_other[at, :] = jnp.where(left, back[:, HALF:], back[:, :HALF])


def weight_kernel(scale, agg_1, agg_2, grad_1, grad_2, chunks, product):
    core = lax.rem(lax.axis_index("row"), 2)
    col = lax.axis_index("col")
    both = (((0,), (0,)), ((), ()))
    product[...] = lax.dot_general(agg_1[...], grad_1[...], both, preferred_element_type=F32)
    product[...] += lax.dot_general(agg_2[...], grad_2[...], both, preferred_element_type=F32)
    bias_sum = jnp.sum(grad_1[...].astype(F32), axis=0, keepdims=True)
    bias_sum = (bias_sum + jnp.sum(grad_2[...].astype(F32), axis=0, keepdims=True)) * scale
    row = lax.broadcasted_iota(jnp.int32, (TAIL, HALF), 0)
    tail = jnp.where(row == 0, bias_sum[:, :HALF], jnp.where(row == 1, bias_sum[:, HALF:], 0.0)).astype(BF)
    for far in range(2):
        for d in range(4):
            for y in range(2):
                rows = product[share_rows(lax.rem(core + far, 2), lax.rem(col // 2 + d, 4), lax.rem(col + y, 2)), :]
                rows = (rows * scale).astype(BF)
                chunks[far, d, y, :SHARE, :] = rows[:, :HALF]
                chunks[far, d, y, SHARE : 2 * SHARE, :] = rows[:, HALF:]
                chunks[far, d, y, 2 * SHARE :, :] = tail


def share_rows(core, z, y):
    return pl.ds(pl.multiple_of((core * 8 + z * 2 + y) * SHARE, SHARE), SHARE)


def place_kernel(own, moved_1, moved_2, moved_3, weight_grad, bias_grad):
    core = lax.rem(lax.axis_index("row"), 2)
    col = lax.axis_index("col")
    for d, piece in enumerate((own, moved_1, moved_2, moved_3)):
        for y in range(2):
            for far in range(2):
                at = share_rows(lax.rem(core + far, 2), lax.rem(col // 2 + 4 - d, 4), lax.rem(col + y, 2))
                weight_grad[at, :HALF] = piece[far, y, :SHARE, :].astype(F32)
                weight_grad[at, HALF:] = piece[far, y, SHARE : 2 * SHARE, :].astype(F32)
    bias_grad[:, :HALF] = own[0, 0, 2 * SHARE : 2 * SHARE + 1, :].astype(F32)
    bias_grad[:, HALF:] = own[0, 0, 2 * SHARE + 1 : 2 * SHARE + 2, :].astype(F32)


def final_kernel(first_mine, first_other, rest_mine, rest_other, out):
    left = lax.axis_index("row") % 2 == 0
    for rows, mine, other in ((slice(0, FIRST), first_mine, first_other), (slice(FIRST, 512), rest_mine, rest_other)):
        a, b = mine[...], other[...]
        out[rows, :HALF] = jnp.where(left, a, b)
        out[rows, HALF:] = jnp.where(left, b, a)


def any_spec():
    return pl.BlockSpec(memory_space=pl.ANY)


def vmem_spec():
    return pl.BlockSpec(memory_space=pltpu.VMEM)


def call(kernel, args, out_shape, ids=(), in_specs=None, scratch=(), flops=0, moved=4 * 2**20, vmem=8 * 2**20):
    shapes = [jax.ShapeDtypeStruct(s, d) for s, d in out_shape]
    return pl.pallas_call(
        kernel,
        grid_spec=pltpu.PrefetchScalarGridSpec(
            num_scalar_prefetch=len(ids),
            in_specs=in_specs or [vmem_spec() for _ in args],
            out_specs=[vmem_spec() for _ in shapes],
            scratch_shapes=scratch,
        ),
        out_shape=shapes,
        compiler_params=pltpu.CompilerParams(vmem_limit_bytes=vmem),
        cost_estimate=pl.CostEstimate(flops=flops, bytes_accessed=moved, transcendentals=0),
    )(*ids, *args)


def core_swap(value):
    return lax.ppermute(value, "row", [(i, i ^ 1) for i in range(16)])


def swap_y(value, high, low):
    to = [(i, i ^ (64 * high + low)) for i in range(128)]
    return lax.ppermute(value, ("row", "col"), to)


def shift(value, axis, d):
    if axis == "row":
        to = [(i, i // 8 * 8 + (i + 2 * d) % 8) for i in range(16)]
    else:
        to = [(i, (i + 2 * d) % 8) for i in range(8)]
    return lax.ppermute(value, axis, to)


def add(*parts):
    total = parts[0].astype(F32)
    for part in parts[1:]:
        total = total + part.astype(F32)
    return total.astype(BF)


def ring(part, axis):
    return (part, *(shift(part, axis, d) for d in range(1, 4)))


def two_way_gather(first, rest, axis, chunks=None):
    high, low = (1, 0) if axis == "row" else (0, 1)
    near = jnp.stack(ring(rest, axis))
    if chunks is None:
        other = swap_y(first, high, low)
    else:
        moved = swap_y(jnp.concatenate([first, chunks[:, 1].reshape(2, 2 * CHUNK, HALF)], axis=1), high, low)
        other = moved[:, :FIRST]
        chunks = add(chunks[:, 0], moved[:, FIRST:].reshape(4, CHUNK, HALF))
    first = jnp.stack([first, other])
    first, near, chunks = lax.optimization_barrier((first, near, chunks))
    far = swap_y(near, high, low)
    if chunks is None:
        pieces = ring(first, axis)
    else:
        flat = first.reshape(-1, HALF)
        size = flat.shape[0]
        moved = [shift(jnp.concatenate([flat, chunks[d]]), axis, d) for d in range(1, 4)]
        pieces = (first, *(part[:size].reshape(first.shape) for part in moved))
        chunks = add(chunks[0], *(part[size:] for part in moved))
    return jnp.concatenate([jnp.stack(pieces), jnp.stack([near, far], axis=1)], axis=3), chunks


def two_way_scatter(parts, axis, chunk=None):
    stay_first, over_y, stay_rest, *ahead = parts
    high, low = (1, 0) if axis == "row" else (0, 1)
    if chunk is None:
        from_y = swap_y(over_y, high, low)
    else:
        flat = over_y.reshape(-1, HALF)
        size = flat.shape[0]
        moved = swap_y(jnp.concatenate([flat, chunk]), high, low)
        from_y = moved[:size].reshape(over_y.shape)
        chunk = add(chunk, moved[size:])
    moved = [shift(part, axis, d + 1) for d, part in enumerate(ahead)]
    rest = [add(stay_rest[y], *(part[y] for part in moved)) for y in range(2)]
    first = [add(stay_first[d], from_y[d]) for d in range(4)]
    first, rest = lax.optimization_barrier((first, rest))
    first = add(first[0], *(shift(first[d], axis, d) for d in range(1, 4)))
    rest = add(rest[0], swap_y(rest[1], high, low))
    return (first[0], core_swap(first[1])), (rest[0], core_swap(rest[1])), chunk


def on_device(features, weight, bias, cotangent, tile_values, tile_rows, tile_cols, tile_counts):
    tiles = tile_values.reshape(64, 128, 128)
    ids = jnp.concatenate([tile_cols.reshape(64), tile_rows.reshape(64), tile_counts.reshape(1)])
    other_tiles, other_ids = core_swap(tiles), core_swap(ids)
    scale = 1.0 / math.sqrt(65536)
    tables = (ids, other_ids)
    def multiply(transposed, source):
        rest = 512 - FIRST
        return call(
            functools.partial(tiles_kernel, transposed),
            (tiles, other_tiles, source),
            [((4, 2, FIRST, HALF), BF)] * 2 + [((2, 2, rest, HALF), BF)] * 4,
            ids=tables,
            in_specs=[any_spec(), any_spec(), vmem_spec()],
            scratch=[
                pltpu.VMEM((2, 64, 128, 128), BF),
                pltpu.VMEM((65, 128, HALF), F32),
                pltpu.SemaphoreType.DMA((2,)),
            ],
            flops=2 * 64 * 128 * 128 * 512,
            moved=16 * 2**20,
            vmem=TILES_VMEM,
        )

    def dense(start, halves):
        rows = halves[0].shape[0]
        return call(
            functools.partial(dense_kernel, start),
            (*halves, weight, bias.reshape(1, 512), cotangent),
            [((rows, 512), BF), ((rows, HALF), BF), ((rows, HALF), BF), ((rows, 512), BF), ((rows, 512), BF)],
            flops=4 * rows * 512**2,
        )

    mine, other = call(halves_kernel, (features,), [((512, HALF), BF)] * 2)
    pair = jnp.stack([mine, core_swap(other)])
    source, _ = two_way_gather(pair[:, :FIRST], pair[:, FIRST:], "row")
    first, rest, _ = two_way_scatter(multiply(False, source), "col")
    rest_output, mine, other, rest_agg, rest_grad = dense(FIRST, rest)
    rest = jnp.stack([mine, core_swap(other)])
    first_output, mine, other, first_agg, first_grad = dense(0, first)
    first = jnp.stack([mine, core_swap(other)])
    output = jnp.concatenate([first_output, rest_output])
    (chunks,) = call(
        functools.partial(weight_kernel, scale),
        (first_agg, rest_agg, first_grad, rest_grad),
        [((2, 4, 2, CHUNK, HALF), BF)],
        scratch=[pltpu.VMEM((512, 512), F32)],
        flops=2 * 512**3,
    )
    chunks = add(chunks[0], core_swap(chunks[1]))
    source, chunk = two_way_gather(first, rest, "col", chunks)
    source, chunk = lax.optimization_barrier((source, chunk))
    parts = multiply(True, source)
    chunk, parts = lax.optimization_barrier((add(*ring(chunk, "row")), parts))
    first, rest, chunk = two_way_scatter(parts, "row", chunk)
    chunks = jnp.stack([chunk, swap_y(chunk, 0, 1)])
    chunks = jnp.stack([chunks, core_swap(chunks)])
    weight_grad, bias_grad = call(place_kernel, ring(chunks, "col"), [((512, 512), F32), ((1, 512), F32)])
    (feature_grad,) = call(final_kernel, (*first, *rest), [((512, 512), BF)])
    return (output, feature_grad, weight_grad, bias_grad.reshape(512))


def solution(mesh):
    return jax.shard_map(
        on_device,
        mesh=mesh,
        in_specs=(
            P(("row", "col"), None),
            P(),
            P(),
            P(("row", "col"), None),
            P("row", "col", None, None, None),
            P("row", "col", None),
            P("row", "col", None),
            P("row", "col"),
        ),
        out_specs=(P(("row", "col"), None), P(("row", "col"), None), P(), P()),
        check_vma=False,
    )
```
